256 devices in a mesh: tm: 128 (over x, z, y_lo, core), batch: 2 (over y_hi).
Axes of the slice: x: 4, y: 4 (y_hi: 2, y_lo: 2; y = y_hi * 2 + y_lo), z: 8, core: 2. Of those that a mesh axis runs over, the one named last changes fastest.
Arguments:
- stem_pre: bfloat16 [2, 16384, 1280], P('batch', 'tm'), may hold values from -6 to 6
- attention_norm_gain: float32 [1280], replicated, may hold values from 0.5 to 1.5
- attention_norm_bias: float32 [1280], replicated, may hold values from -3 to 3
- w_attn: bfloat16 [1280, 2560], replicated, may hold values from -0.15625 to 0.15625
- queries: bfloat16 [2, 16384, 640], P('batch', 'tm'), may hold values from -10 to 10
- keys: bfloat16 [2, 16384, 640], P('batch', 'tm'), may hold values from -4 to 4
- values: bfloat16 [2, 16384, 640], P('batch', 'tm'), may hold values from -6 to 6
- grad_out: bfloat16 [2, 16384, 1280], P('batch', 'tm'), may hold values from -24 to 24
- frames: int32 [2, 8], P('batch'), may hold values from 2048 to 4096, as said below
Outputs:
- grad_stem: bfloat16 [2, 16384, 1280], P('batch', 'tm')
- grad_attn: float32 [1280, 2560], P('tm')
- ln_grads: float32 [2, 1280], replicated
The draws below stay inside these ranges and needn't reach their ends.
Inputs may be any that keep to these rules, and one draw needn't show every extreme that they name: `frames`: one entry per recording, batch row first.
All inputs are finite; a program needn't handle non-finite values.
Results may differ from the reference program's by a relative error of at most 0.02.
Values may be sent and summed in bfloat16 or wider, within the bound.
A program may use at most 128 MiB of HBM per device.

```python
import math
import jax
import jax.numpy as jnp
from jax import lax

D = 1280
HEAD_DIM = 64
HEADS = 10
SPAN = 16
HH = 640
SEQ = 2048
TOKENS = 16384
N_TM = 128
N_BATCH = 2


def pair_base(key, align_on):
    full_shape = (N_BATCH, TOKENS, HH)
    key_query, key_key, key_pick = jax.random.split(key, 3)
    normal_query = jnp.clip(jax.random.normal(key_query, full_shape, jnp.float32), -3.5, 3.5)
    normal_key = jnp.clip(jax.random.normal(key_key, full_shape, jnp.float32), -3.5, 3.5)
    base_query = normal_query
    base_key = normal_key
    picked_rows = jax.random.randint(key_pick, (N_BATCH, TOKENS // SEQ, 4), 0, SEQ // 2 - 1)
    row_ids = jnp.arange(TOKENS)
    within = row_ids % SEQ
    owner_group = row_ids // SEQ
    chosen = picked_rows[:, owner_group, :]
    aligned = jnp.any(within[None, :, None] == chosen, axis=-1) & (align_on > 0.0)
    twin_rows = jnp.roll(aligned, 1, axis=1)
    strength = 1.0 + 0.75 * (within % 3).astype(jnp.float32)
    peak_keys = jnp.where(base_key >= 0.0, 4.0, -4.0)
    keys_out = jnp.where(aligned[:, :, None], peak_keys, jnp.where(twin_rows[:, :, None], 0.992 * jnp.roll(peak_keys, 1, axis=1), base_key))
    queries_out = jnp.where(aligned[:, :, None], strength[None, :, None] * peak_keys, base_query)
    return (queries_out, keys_out)


def draw_queries(key, part):
    shared = pair_base(key, 0.0)
    return shared[0].astype(jnp.bfloat16)


def draw_keys(key, part):
    shared = pair_base(key, 0.0)
    return shared[1].astype(jnp.bfloat16)


def draw_frames(key, part):
    key = jax.random.fold_in(key, 11)
    key_counts, key_spot = jax.random.split(key)
    group_count = N_TM // SPAN
    frame_counts = jax.random.randint(key_counts, (N_BATCH * group_count,), SEQ, 2 * SEQ + 1)
    spot_index = jax.random.randint(key_spot, (), 0, N_BATCH * group_count)
    flat_counts = jnp.where(jnp.arange(N_BATCH * group_count) == spot_index, 2 * SEQ, frame_counts)
    return flat_counts.reshape(N_BATCH, group_count).astype(jnp.int32)


def strengthened(drawn, own_key, source, target, blocks, factor):
    def block_of(position):
        return (jnp.arange(drawn.shape[position]) // (drawn.shape[position] // blocks)).reshape((-1,) + (1,) * (drawn.ndim - 1 - position))

    near = jax.random.permutation(own_key, blocks)[block_of(target)]
    other_side = (block_of(target) + blocks // 2) % blocks
    return jnp.where((block_of(source) == near) | (block_of(source) == other_side), factor * drawn, drawn)


def block_scale(key, dims, cuts, low, top_value):
    factor_of = 1.0
    for axis_at, shards_of in cuts:
        steps = jax.random.uniform(jax.random.fold_in(jax.random.fold_in(key, 6), axis_at), (shards_of,), jnp.float32, low / len(cuts), top_value / len(cuts))
        factor_of = factor_of * jnp.repeat(jnp.exp(steps), dims[axis_at] // shards_of).reshape((-1,) + (1,) * (len(dims) - 1 - axis_at))
    return factor_of


def scatter_about(own_key, extent, scale, bound, pieces=(), kind=jnp.bfloat16):
    drawn = jax.random.normal(own_key, extent, jnp.float32) * scale
    if len(pieces) > 0:
        drawn = block_scale(own_key, extent, pieces, -0.22, 0.18) * drawn
    return jnp.clip(drawn, min=-bound, max=bound).astype(kind)


def noise_with(rng, shape, width, reach, pieces, heavy, kind=jnp.bfloat16):
    values = width * jax.random.normal(rng, shape, jnp.float32)
    if pieces:
        values = values * block_scale(rng, shape, pieces, -0.22, 0.18)
    return jnp.clip(strengthened(values, jax.random.fold_in(rng, 3), *heavy), -reach, reach).astype(kind)


def setup_inputs(seed: int = 0) -> dict:
    seeds = jax.random.split(jax.random.key(seed), 10)
    stem_pre = scatter_about(seeds[0], (N_BATCH, TOKENS, D), 1.0, 6.0, ((0, 2), (1, 128)))
    attention_norm_gain = jnp.clip(1.0 + 0.1 * jax.random.normal(seeds[1], (D,), jnp.float32), 0.5, 1.5)
    attention_norm_bias = scatter_about(seeds[2], (D,), 0.5, 3.0, (), jnp.float32)
    w_attn = scatter_about(seeds[3], (D, 4 * HH), D ** -0.5, 0.15625)
    queries = draw_queries(jax.random.fold_in(seeds[9], 71), 0)
    keys = draw_keys(jax.random.fold_in(seeds[9], 71), 0)
    values = scatter_about(seeds[6], (N_BATCH, TOKENS, HH), 1.0, 6.0, ((0, 2), (1, 128)))
    grad_out = noise_with(seeds[7], (N_BATCH, TOKENS, D), 1.0, 24.0, ((0, 2), (1, 128)), (1, 2, 128, 5.5))
    frames = draw_frames(jax.random.fold_in(seeds[9], 71), 0)
    return {"stem_pre": stem_pre, "attention_norm_gain": attention_norm_gain, "attention_norm_bias": attention_norm_bias, "w_attn": w_attn, "queries": queries, "keys": keys, "values": values, "grad_out": grad_out, "frames": frames}


NEG_FILL = -1e+30
EPSILON = 1e-05

def gelu_and_slope(stem_in):
    normal_cdf = 0.5 * (1.0 + lax.erf(stem_in / math.sqrt(2.0)))
    density = jnp.exp(-0.5 * stem_in * stem_in) / math.sqrt(2.0 * math.pi)
    return (stem_in * normal_cdf, normal_cdf + stem_in * density)

def sinusoid(positions, features):
    half_width = features // 2
    frequency = jnp.exp(-math.log(10000.0) / (half_width - 1) * jnp.arange(half_width, dtype=jnp.float32))
    angles = positions[:, None] * frequency[None, :]
    return jnp.concatenate([jnp.sin(angles), jnp.cos(angles)], axis=1)

def layer_backward(stem_raw, query_raw, key_raw, value_raw, incoming_gradient, frame_limit, attention_norm_gain, attention_norm_bias, w_attn):
    scale = 1.0 / math.sqrt(HEAD_DIM)
    stem_in = stem_raw.astype(jnp.float32)
    activated, gelu_slope = gelu_and_slope(stem_in)
    embedded = activated + sinusoid(jnp.arange(SEQ, dtype=jnp.float32), D)
    row_mean = lax.optimization_barrier(jnp.mean(embedded, axis=1, keepdims=True))
    centered_input = embedded - row_mean
    inverse_deviation = lax.rsqrt(lax.optimization_barrier(jnp.mean(centered_input * centered_input, axis=1, keepdims=True)) + EPSILON)
    standardized_input = centered_input * inverse_deviation
    normalized_input = (standardized_input * attention_norm_gain + attention_norm_bias).astype(jnp.bfloat16)
    w_qkv = w_attn[:, :3 * HH]
    w_outt = w_attn[:, 3 * HH:]
    grad_heads = jnp.dot(incoming_gradient, w_outt, preferred_element_type=jnp.float32).astype(jnp.bfloat16)
    key_valid = 2 * jnp.arange(SEQ) < frame_limit
    query_heads = query_raw.astype(jnp.float32).reshape(SEQ, HEADS, HEAD_DIM)
    key_heads = key_raw.astype(jnp.float32).reshape(SEQ, HEADS, HEAD_DIM)
    value_heads = value_raw.astype(jnp.float32).reshape(SEQ, HEADS, HEAD_DIM)
    cot_heads = grad_heads.astype(jnp.float32).reshape(SEQ, HEADS, HEAD_DIM)
    scores = jnp.einsum('qhd,khd->hqk', query_heads, key_heads) * scale
    scores = jnp.where(key_valid[None, None, :], scores, NEG_FILL)
    totals = jax.nn.logsumexp(scores, axis=2)
    attn_prob = jnp.exp(scores - totals[:, :, None])
    prob_bf = attn_prob.astype(jnp.bfloat16).astype(jnp.float32)
    attn_out = jnp.einsum('hqk,khd->qhd', prob_bf, value_heads).reshape(SEQ, HH).astype(jnp.bfloat16)
    row_delta = jnp.einsum('qhd,qhd->hq', cot_heads, attn_out.astype(jnp.float32).reshape(SEQ, HEADS, HEAD_DIM))
    grad_prob = jnp.einsum('qhd,khd->hqk', cot_heads, value_heads)
    dscore = (attn_prob * (grad_prob - row_delta[:, :, None]) * scale).astype(jnp.bfloat16).astype(jnp.float32)
    grad_query = jnp.einsum('hqk,khd->qhd', dscore, key_heads).reshape(SEQ, HH)
    grad_key = jnp.einsum('hqk,qhd->khd', dscore, query_heads).reshape(SEQ, HH)
    grad_value = jnp.einsum('hqk,qhd->khd', prob_bf, cot_heads).reshape(SEQ, HH)
    grad_qkv = jnp.concatenate([grad_query, grad_key, grad_value], axis=1).astype(jnp.bfloat16)
    normalized_gradient = lax.dot_general(grad_qkv, w_qkv, (((1,), (1,)), ((), ())), preferred_element_type=jnp.float32)
    weight_part = jnp.concatenate([lax.dot_general(normalized_input, grad_qkv, (((0,), (0,)), ((), ())), preferred_element_type=jnp.float32), lax.dot_general(incoming_gradient, attn_out, (((0,), (0,)), ((), ())), preferred_element_type=jnp.float32)], axis=1)
    norm_component = jnp.stack([lax.optimization_barrier(jnp.sum(normalized_gradient * standardized_input, axis=0)), lax.optimization_barrier(jnp.sum(normalized_gradient, axis=0))])
    gain_scaled_gradient = normalized_gradient * attention_norm_gain
    input_gradient = incoming_gradient.astype(jnp.float32) + inverse_deviation * (gain_scaled_gradient - lax.optimization_barrier(jnp.mean(gain_scaled_gradient, axis=1, keepdims=True)) - standardized_input * lax.optimization_barrier(jnp.mean(gain_scaled_gradient * standardized_input, axis=1, keepdims=True)))
    return ((input_gradient * gelu_slope).astype(jnp.bfloat16), weight_part, norm_component)

def reference(stem_pre, attention_norm_gain, attention_norm_bias, w_attn, queries, keys, values, grad_out, frames):
    count = N_BATCH * (TOKENS // SEQ)

    def by_recording(array):
        return array.reshape(count, SEQ, array.shape[-1])

    def accumulate(totals, record):
        stem_raw, query_raw, key_raw, value_raw, incoming_gradient, frame_limit = record
        grad_piece, weight_part, norm_component = layer_backward(stem_raw, query_raw, key_raw, value_raw, incoming_gradient, frame_limit, attention_norm_gain, attention_norm_bias, w_attn)
        return ((totals[0] + weight_part, totals[1] + norm_component), grad_piece)
    start_totals = (jnp.zeros((D, 4 * HH), jnp.float32), jnp.zeros((2, D), jnp.float32))
    records = (by_recording(stem_pre), by_recording(queries), by_recording(keys), by_recording(values), by_recording(grad_out), frames.reshape(-1))
    (grad_attn, ln_grads), grad_pieces = lax.scan(accumulate, start_totals, records)
    return (grad_pieces.reshape(N_BATCH, TOKENS, D), grad_attn, ln_grads)
```

```python
import math

import jax
import jax.numpy as jnp
from jax import lax
from jax.experimental import pallas as pl
from jax.experimental.pallas import tpu as pltpu
from jax.sharding import PartitionSpec as P

HEAD_DIM = 64
HEADS = 10
SPAN = 16


NEG_FILL = -1e30
EPSILON = 1e-05


def gelu_and_slope(stem_in):
    normal_cdf = 0.5 * (1.0 + lax.erf(stem_in / math.sqrt(2.0)))
    density = jnp.exp(-0.5 * stem_in * stem_in) / math.sqrt(2.0 * math.pi)
    return (stem_in * normal_cdf, normal_cdf + stem_in * density)


def sinusoid(positions, features):
    half_width = features // 2
    frequency = jnp.exp(
        -math.log(10000.0) / (half_width - 1) * jnp.arange(half_width, dtype=jnp.float32)
    )
    angles = positions[:, None] * frequency[None, :]
    return jnp.concatenate([jnp.sin(angles), jnp.cos(angles)], axis=1)


OWNERS = (0, 2, 4, 5, 6, 8, 10, 11, 12, 14)
MESH = pl.DeviceIdType.MESH
ROWS = 128
BLOCK = 256


def attention_kernel(
    q_ref, k_ref, v_ref, go_ref, w_ref, frames_ref, out_ref,
    kv_out, qd_out, kv_in, qd_in, ret_qo, ret_kv, got, masked_k, kv_t, total,
    send_kv, send_qd, send_qo, send_dkv, recv_kv, recv_qd, recv_got,
):
    me = lax.axis_index("tm")
    slot = lax.rem(me, SPAN)
    base = me - slot

    barrier = pltpu.get_barrier_semaphore()
    for other in range(1, SPAN):
        peer = base + lax.rem(slot + other, SPAN)
        pl.semaphore_signal(barrier, inc=1, device_id={"tm": peer}, device_id_type=MESH)

    for h in range(HEADS):
        cols = slice(h * HEAD_DIM, (h + 1) * HEAD_DIM)
        kv_out[h] = jnp.concatenate([k_ref[0, :, cols], v_ref[0, :, cols]], axis=1)
    pl.semaphore_wait(barrier, SPAN - 1)

    def to_owner(h, buf, landing, send_sem, recv_sem):
        return pltpu.make_async_remote_copy(
            src_ref=buf.at[h], dst_ref=landing.at[slot],
            send_sem=send_sem.at[h], recv_sem=recv_sem,
            device_id={"tm": base + OWNERS[h]}, device_id_type=MESH,
        )

    def send_heads(buf, landing, send_sem, recv_sem):
        for h in range(HEADS):
            @pl.when(slot != OWNERS[h])
            def _():
                to_owner(h, buf, landing, send_sem, recv_sem).start()

            @pl.when(slot == OWNERS[h])
            def _():
                pltpu.make_async_copy(buf.at[h], landing.at[slot], recv_sem).start()

    send_heads(kv_out, kv_in, send_kv, recv_kv)
    grad_heads = jnp.dot(go_ref[0], w_ref[...], preferred_element_type=jnp.float32).astype(jnp.bfloat16)
    for h in range(HEADS):
        cols = slice(h * HEAD_DIM, (h + 1) * HEAD_DIM)
        qd_out[h] = jnp.concatenate([q_ref[0, :, cols], grad_heads[:, cols]], axis=1)
    send_heads(qd_out, qd_in, send_qd, recv_qd)

    head = jnp.int32(0)
    active = jnp.bool_(False)
    for h in range(HEADS):
        head = jnp.where(slot == OWNERS[h], h, head)
        active = jnp.logical_or(active, slot == OWNERS[h])
    seq = SPAN * ROWS

    def back(buf, index, part, send_sem):
        return pltpu.make_async_remote_copy(
            src_ref=buf.at[index], dst_ref=got.at[part, head],
            send_sem=send_sem.at[index], recv_sem=recv_got,
            device_id={"tm": base + index}, device_id_type=MESH,
        )

    def send_back(buf, index, part, send_sem):
        @pl.when(slot != index)
        def _():
            back(buf, index, part, send_sem).start()

        @pl.when(slot == index)
        def _():
            pltpu.make_async_copy(buf.at[index], got.at[part, head], recv_got).start()

    @pl.when(active)
    def _():
        limit = frames_ref[0, me // SPAN]
        pltpu.make_async_copy(kv_in, kv_in, recv_kv).wait()
        kv = kv_in[...].reshape(seq, 2 * HEAD_DIM)
        lane = lax.broadcasted_iota(jnp.int32, kv.shape, 1)
        row = lax.broadcasted_iota(jnp.int32, kv.shape, 0)
        fill = jnp.where(jnp.logical_and(lane == HEAD_DIM, 2 * row >= limit), NEG_FILL, 0.0)
        masked_k[...] = jnp.where(lane < HEAD_DIM, kv.astype(jnp.float32), fill).astype(jnp.bfloat16)
        kv_t[...] = kv.T
        total[...] = jnp.zeros_like(total)
        pltpu.make_async_copy(qd_in, qd_in, recv_qd).wait()
        scale = 1.0 / math.sqrt(HEAD_DIM)
        blane = lax.broadcasted_iota(jnp.int32, (BLOCK, 2 * HEAD_DIM), 1)
        brow = lax.broadcasted_iota(jnp.int32, (2 * HEAD_DIM, BLOCK), 0)

        def body(i, carry):
            qd = qd_in[pl.ds(2 * i, 2)].reshape(BLOCK, 2 * HEAD_DIM).astype(jnp.float32)
            q_ones = jnp.where(blane < HEAD_DIM, qd * scale, jnp.where(blane == HEAD_DIM, 1.0, 0.0)).astype(jnp.bfloat16)
            q_only = jnp.where(blane < HEAD_DIM, qd, 0.0).astype(jnp.bfloat16)
            d_only = jnp.where(blane >= HEAD_DIM, qd, 0.0).astype(jnp.bfloat16)
            scores = lax.dot_general(
                masked_k[...], q_ones, (((1,), (1,)), ((), ())), preferred_element_type=jnp.float32
            )
            top = jnp.max(scores, axis=0, keepdims=True)
            power = jnp.exp(scores - top)
            prob = power * (1.0 / jnp.sum(power, axis=0, keepdims=True))
            prob_b = prob.astype(jnp.bfloat16)
            attn_t = jnp.dot(kv_t[...], prob_b, preferred_element_type=jnp.float32)
            attn_t = attn_t.astype(jnp.bfloat16).astype(jnp.float32)
            delta = jnp.sum(jnp.where(brow >= HEAD_DIM, qd.T * attn_t, 0.0), axis=0, keepdims=True)
            grad_prob = lax.dot_general(
                kv_in[...].reshape(seq, 2 * HEAD_DIM), d_only, (((1,), (1,)), ((), ())), preferred_element_type=jnp.float32
            )
            dscore = (prob * (grad_prob - delta) * scale).astype(jnp.bfloat16)
            dq_t = jnp.dot(kv_t[...], dscore, preferred_element_type=jnp.float32)
            result = jnp.where(brow < HEAD_DIM, dq_t, attn_t).T.astype(jnp.bfloat16)
            ret_qo[pl.ds(2 * i, 2)] = result.reshape(2, ROWS, 2 * HEAD_DIM)
            send_back(ret_qo, 2 * i, 0, send_qo)
            send_back(ret_qo, 2 * i + 1, 0, send_qo)
            total[...] += jnp.dot(dscore, q_only, preferred_element_type=jnp.float32) + jnp.dot(
                prob_b, d_only, preferred_element_type=jnp.float32
            )
            return carry

        lax.fori_loop(0, seq // BLOCK, body, 0)
        ret_kv[...] = total[...].astype(jnp.bfloat16).reshape(SPAN, ROWS, 2 * HEAD_DIM)

        def send_kv_grads(i, carry):
            send_back(ret_kv, i, 1, send_dkv)
            return carry

        lax.fori_loop(0, SPAN, send_kv_grads, 0)

    pltpu.make_async_copy(got, got, recv_got).wait()
    for h in range(HEADS):
        for part, (left, right) in enumerate(((0, 3), (1, 2))):
            tile = got[part, h]
            out_ref[:, left * HEADS * HEAD_DIM + h * HEAD_DIM : left * HEADS * HEAD_DIM + (h + 1) * HEAD_DIM] = tile[:, :HEAD_DIM]
            out_ref[:, right * HEADS * HEAD_DIM + h * HEAD_DIM : right * HEADS * HEAD_DIM + (h + 1) * HEAD_DIM] = tile[:, HEAD_DIM:]

    for h in range(HEADS):
        @pl.when(slot != OWNERS[h])
        def _():
            to_owner(h, kv_out, kv_in, send_kv, recv_kv).wait_send()
            to_owner(h, qd_out, qd_in, send_qd, recv_qd).wait_send()

    @pl.when(active)
    def _():
        def drain(i, carry):
            @pl.when(slot != i)
            def _():
                back(ret_qo, i, 0, send_qo).wait_send()
                back(ret_kv, i, 1, send_dkv).wait_send()
            return carry

        lax.fori_loop(0, SPAN, drain, 0)


def attention_exchange(queries, keys, values, grad_out, w_attn, frames):
    width = HEADS * HEAD_DIM
    rows, features = grad_out.shape[1:]
    tile = (ROWS, 2 * HEAD_DIM)
    seq = SPAN * ROWS
    vmem = pltpu.VMEM
    return pl.pallas_call(
        attention_kernel,
        grid=(1,),
        out_shape=jax.ShapeDtypeStruct((rows, 4 * width), jnp.bfloat16),
        in_specs=[
            pl.BlockSpec((1, rows, width), lambda i: (0, 0, 0)),
            pl.BlockSpec((1, rows, width), lambda i: (0, 0, 0)),
            pl.BlockSpec((1, rows, width), lambda i: (0, 0, 0)),
            pl.BlockSpec((1, rows, features), lambda i: (0, 0, 0)),
            pl.BlockSpec((features, width), lambda i: (0, 3)),
            pl.BlockSpec(memory_space=pltpu.SMEM),
        ],
        out_specs=pl.BlockSpec((rows, 4 * width), lambda i: (0, 0)),
        scratch_shapes=[
            vmem((HEADS,) + tile, jnp.bfloat16),
            vmem((HEADS,) + tile, jnp.bfloat16),
            vmem((SPAN,) + tile, jnp.bfloat16),
            vmem((SPAN,) + tile, jnp.bfloat16),
            vmem((SPAN,) + tile, jnp.bfloat16),
            vmem((SPAN,) + tile, jnp.bfloat16),
            vmem((2, HEADS) + tile, jnp.bfloat16),
            vmem((seq, 2 * HEAD_DIM), jnp.bfloat16),
            vmem((2 * HEAD_DIM, seq), jnp.bfloat16),
            vmem((seq, 2 * HEAD_DIM), jnp.float32),
            pltpu.SemaphoreType.DMA((HEADS,)),
            pltpu.SemaphoreType.DMA((HEADS,)),
            pltpu.SemaphoreType.DMA((SPAN,)),
            pltpu.SemaphoreType.DMA((SPAN,)),
            pltpu.SemaphoreType.DMA,
            pltpu.SemaphoreType.DMA,
            pltpu.SemaphoreType.DMA,
        ],
        compiler_params=pltpu.CompilerParams(
            collective_id=0, has_side_effects=True, vmem_limit_bytes=50 * 1024 * 1024
        ),
        name="attention_exchange",
    )(queries, keys, values, grad_out, w_attn, frames)


N_X, N_Z, QUAD, N_Y = 4, 8, 4, 2
PIECE = 640
X_ROWS = 320
HALF = 160
Z_ROWS = 40
Z_PAD = 48
OUT_ROWS = 10
OUT_PAD = 16


def weight_kernel(
    normed_ref, go_ref, cols_ref, norm_ref, out_ref, norm_out_ref,
    left, right, wide, sends, first, joined, alone, joint_out, z_out, z_in, last_out, last_in,
    norm_a, norm_b, norm_c, norm_mid,
    s_left, s_right, s_first, s_joined, s_alone, s_z, s_last, s_na, s_nb, s_nc,
    r_left, r_right, r_first, r_joined, r_alone, r_z, r_last, r_na, r_nb, r_nc,
):
    me = lax.axis_index("tm")
    side = lax.axis_index("batch")
    t = lax.rem(me, QUAD)
    z = lax.rem(me // QUAD, N_Z)
    x = me // (QUAD * N_Z)
    mine8 = side * QUAD + t

    def at_x(step):
        return {"tm": lax.rem(x + step, N_X) * (QUAD * N_Z) + z * QUAD + t}

    def at_z(step):
        return {"tm": x * (QUAD * N_Z) + lax.rem(z + step, N_Z) * QUAD + t}

    def at_quad(step):
        return {"tm": x * (QUAD * N_Z) + z * QUAD + lax.rem(t + step, QUAD)}

    def at_eight(step):
        place = lax.rem(mine8 + step, 2 * QUAD)
        return {"tm": x * (QUAD * N_Z) + z * QUAD + lax.rem(place, QUAD), "batch": place // QUAD}

    def remote(src, dst, send_sem, recv_sem, device):
        return pltpu.make_async_remote_copy(
            src_ref=src, dst_ref=dst, send_sem=send_sem, recv_sem=recv_sem,
            device_id=device, device_id_type=MESH,
        )

    def landed(buf, sem):
        pltpu.make_async_copy(buf, buf, sem).wait()

    barrier = pltpu.get_barrier_semaphore()
    for step in range(1, N_X):
        pl.semaphore_signal(barrier, inc=1, device_id=at_x(step), device_id_type=MESH)
    for step in range(1, N_Z):
        pl.semaphore_signal(barrier, inc=1, device_id=at_z(step), device_id_type=MESH)
    for step in range(1, 2 * QUAD):
        pl.semaphore_signal(barrier, inc=1, device_id=at_eight(step), device_id_type=MESH)
    pl.semaphore_wait(barrier, N_X - 1 + N_Z - 1 + 2 * QUAD - 1)

    pending = []

    def go(copy):
        copy.start()
        pending.append(copy)

    for step in range(1, QUAD):
        other = lax.rem(t + step, QUAD)
        columns = pl.ds(pl.multiple_of(other * PIECE, 128), PIECE)
        go(remote(cols_ref.at[:, columns], right.at[t], s_right.at[step], r_right, at_quad(step)))
    own_columns = pl.ds(pl.multiple_of(t * PIECE, 128), PIECE)
    pltpu.make_async_copy(cols_ref.at[:, own_columns], right.at[t], r_right).start()
    for step in range(1, QUAD):
        other = lax.rem(t + step, QUAD)
        from_normed = remote(normed_ref, left.at[t], s_left.at[step], r_left, at_quad(step))
        from_go = remote(go_ref.at[0], left.at[t], s_left.at[step], r_left, at_quad(step))
        pl.when(other < QUAD - 1)(from_normed.start)
        pl.when(other == QUAD - 1)(from_go.start)
        pending.append(from_normed)
    pl.when(t < QUAD - 1)(pltpu.make_async_copy(normed_ref, left.at[t], r_left).start)
    pl.when(t == QUAD - 1)(pltpu.make_async_copy(go_ref.at[0], left.at[t], r_left).start)

    for step in range(1, N_Z):
        go(remote(norm_ref, norm_a.at[z], s_na.at[step], r_na, at_z(step)))
    pltpu.make_async_copy(norm_ref, norm_a.at[z], r_na).start()
    landed(norm_a, r_na)
    norm_mid[0] = jnp.sum(norm_a[...], axis=0)
    for step in range(1, N_X):
        go(remote(norm_mid.at[0], norm_b.at[x], s_nb.at[step], r_nb, at_x(step)))
    pltpu.make_async_copy(norm_mid.at[0], norm_b.at[x], r_nb).start()
    landed(norm_b, r_nb)
    norm_mid[1] = jnp.sum(norm_b[...], axis=0)
    for step in range(1, 2 * QUAD):
        go(remote(norm_mid.at[1], norm_c.at[mine8], s_nc.at[step], r_nc, at_eight(step)))
    pltpu.make_async_copy(norm_mid.at[1], norm_c.at[mine8], r_nc).start()

    landed(right, r_right)
    landed(left, r_left)
    tokens = QUAD * ROWS
    features = N_X * X_ROWS
    for at in range(0, features, 256):
        product = lax.dot_general(
            left[:, :, at : at + 256].reshape(tokens, 256),
            right[...].reshape(tokens, PIECE),
            (((0,), (0,)), ((), ())),
            preferred_element_type=jnp.float32,
        )
        wide[at : at + 256] = product
        sends[at : at + 256] = product.astype(jnp.bfloat16)

    def rows_of(step, half):
        chunk = lax.rem(x + step, N_X)
        return pl.ds(pl.multiple_of(chunk * X_ROWS + half * HALF, 32), HALF)

    for half, step in ((0, 1), (1, N_X - 1)):
        go(remote(sends.at[rows_of(2, half)], first.at[half], s_first.at[half], r_first.at[half], at_x(step)))
    for half, step in ((0, 1), (1, N_X - 1)):
        go(remote(sends.at[rows_of(step, 1 - half)], alone.at[1 - half], s_alone.at[half], r_alone.at[1 - half], at_x(step)))
    for half, step in ((0, 1), (1, N_X - 1)):
        landed(first.at[half], r_first.at[half])
        joint_out[half] = (first[half].astype(jnp.float32) + wide[rows_of(step, half)]).astype(jnp.bfloat16)
        go(remote(joint_out.at[half], joined.at[half], s_joined.at[half], r_joined.at[half], at_x(step)))

    for half in range(2):
        landed(alone.at[half], r_alone.at[half])
        landed(joined.at[half], r_joined.at[half])
        total = wide[rows_of(0, half)] + alone[half].astype(jnp.float32) + joined[half].astype(jnp.float32)
        for part in range(HALF // Z_ROWS):
            z_out[half * (HALF // Z_ROWS) + part] = jnp.concatenate(
                [total[part * Z_ROWS : (part + 1) * Z_ROWS], jnp.zeros((Z_PAD - Z_ROWS, PIECE), jnp.float32)], axis=0
            ).astype(jnp.bfloat16)
    for step in range(1, N_Z):
        go(remote(z_out.at[lax.rem(z + step, N_Z)], z_in.at[z], s_z.at[step], r_z, at_z(step)))
    pltpu.make_async_copy(z_out.at[z], z_in.at[z], r_z).start()
    landed(norm_c, r_nc)
    norm_out_ref[...] = jnp.sum(norm_c[...], axis=0)
    landed(z_in, r_z)
    total = jnp.sum(z_in[...].astype(jnp.float32), axis=0)[:Z_ROWS]

    for place in range(QUAD):
        last_out[place] = jnp.concatenate(
            [total[place * OUT_ROWS : (place + 1) * OUT_ROWS], jnp.zeros((OUT_PAD - OUT_ROWS, PIECE), jnp.float32)], axis=0
        )
    for step in range(1, 2 * QUAD):
        place = lax.rem(lax.rem(mine8 + step, 2 * QUAD), QUAD)
        go(remote(last_out.at[place], last_in.at[mine8], s_last.at[step], r_last, at_eight(step)))
    pltpu.make_async_copy(last_out.at[t], last_in.at[mine8], r_last).start()
    landed(last_in, r_last)
    for block in range(QUAD):
        both = last_in[block] + last_in[QUAD + block]
        out_ref[:, block * PIECE : (block + 1) * PIECE] = both[:OUT_ROWS]
    for copy in pending:
        copy.wait_send()


def weight_exchange(normed, grad_out, columns, norm_terms):
    rows, features = normed.shape
    vmem, dma = pltpu.VMEM, pltpu.SemaphoreType.DMA
    bf, f32 = jnp.bfloat16, jnp.float32
    return pl.pallas_call(
        weight_kernel,
        out_shape=(
            jax.ShapeDtypeStruct((OUT_ROWS, QUAD * PIECE), f32),
            jax.ShapeDtypeStruct(norm_terms.shape, f32),
        ),
        in_specs=[pl.BlockSpec(memory_space=vmem)] * 4,
        out_specs=(pl.BlockSpec(memory_space=vmem), pl.BlockSpec(memory_space=vmem)),
        scratch_shapes=[
            vmem((QUAD, rows, features), bf),
            vmem((QUAD, rows, PIECE), bf),
            vmem((features, PIECE), f32),
            vmem((features, PIECE), bf),
            vmem((2, HALF, PIECE), bf),
            vmem((2, HALF, PIECE), bf),
            vmem((2, HALF, PIECE), bf),
            vmem((2, HALF, PIECE), bf),
            vmem((N_Z, Z_PAD, PIECE), bf),
            vmem((N_Z, Z_PAD, PIECE), bf),
            vmem((QUAD, OUT_PAD, PIECE), f32),
            vmem((2 * QUAD, OUT_PAD, PIECE), f32),
            vmem((N_Z,) + norm_terms.shape, f32),
            vmem((N_X,) + norm_terms.shape, f32),
            vmem((2 * QUAD,) + norm_terms.shape, f32),
            vmem((2,) + norm_terms.shape, f32),
            dma((QUAD,)), dma((QUAD,)), dma((2,)), dma((2,)), dma((2,)),
            dma((N_Z,)), dma((2 * QUAD,)), dma((N_Z,)), dma((N_X,)), dma((2 * QUAD,)),
            dma, dma, dma((2,)), dma((2,)), dma((2,)), dma, dma, dma, dma, dma,
        ],
        compiler_params=pltpu.CompilerParams(
            collective_id=1, has_side_effects=True, vmem_limit_bytes=50 * 1024 * 1024
        ),
        name="weight_exchange",
    )(normed, grad_out, columns, norm_terms)


def local(
    stem_pre,
    attention_norm_gain,
    attention_norm_bias,
    w_attn,
    queries,
    keys,
    values,
    grad_out,
    frames,
):
    tok_rows = stem_pre.shape[1]
    features = stem_pre.shape[2]
    head_width = queries.shape[2]
    group_slot = lax.axis_index("tm") % SPAN
    offset = group_slot * tok_rows
    stem_in = stem_pre[0].astype(jnp.float32)
    activated, gelu_slope = gelu_and_slope(stem_in)
    positions = (offset + jnp.arange(tok_rows)).astype(jnp.float32)
    embedded = activated + sinusoid(positions, features)
    row_mean = jnp.mean(embedded, axis=1, keepdims=True)
    centered_input = embedded - row_mean
    inverse_deviation = lax.rsqrt(
        jnp.mean(centered_input * centered_input, axis=1, keepdims=True) + EPSILON
    )
    standardized_input = centered_input * inverse_deviation
    normalized_input = (standardized_input * attention_norm_gain + attention_norm_bias).astype(
        jnp.bfloat16
    )
    incoming_gradient = grad_out[0]
    columns = attention_exchange(queries, keys, values, grad_out, w_attn, frames)
    grad_qkv = columns[:, : 3 * head_width]
    normalized_gradient = lax.dot_general(
        grad_qkv,
        w_attn[:, : 3 * head_width],
        (((1,), (1,)), ((), ())),
        preferred_element_type=jnp.float32,
    )
    norm_terms = jnp.stack(
        [
            jnp.sum(normalized_gradient * standardized_input, axis=0),
            jnp.sum(normalized_gradient, axis=0),
        ]
    )
    packed = jnp.pad(norm_terms.reshape(-1, ROWS), ((0, 4), (0, 0)))
    grad_attn, norm_sums = weight_exchange(normalized_input, grad_out, columns, packed)
    ln_grads = norm_sums[: 2 * features // ROWS].reshape(2, features)
    gain_scaled_gradient = normalized_gradient * attention_norm_gain
    input_gradient = incoming_gradient.astype(jnp.float32) + inverse_deviation * (
        gain_scaled_gradient
        - jnp.mean(gain_scaled_gradient, axis=1, keepdims=True)
        - standardized_input
        * jnp.mean(gain_scaled_gradient * standardized_input, axis=1, keepdims=True)
    )
    grad_stem = (input_gradient * gelu_slope).astype(jnp.bfloat16)
    return (grad_stem[None], grad_attn, ln_grads)


def solution(mesh):
    placed = (
        P("batch", "tm", None),
        P(),
        P(),
        P(),
        P("batch", "tm", None),
        P("batch", "tm", None),
        P("batch", "tm", None),
        P("batch", "tm", None),
        P("batch", None),
    )
    return jax.shard_map(
        local,
        mesh=mesh,
        in_specs=placed,
        out_specs=(P("batch", "tm", None), P("tm", None), P()),
        check_vma=False,
    )
```

```python
import math

import jax
import jax.numpy as jnp
from jax import lax
from jax.experimental import pallas as pl
from jax.experimental.pallas import tpu as pltpu
from jax.sharding import PartitionSpec as P

HEAD_DIM = 64
HEADS = 10
SPAN = 16
NEG_FILL = -1e30
EPSILON = 1e-05

OWNERS = (0, 4, 5, 8, 12, 2, 6, 10, 11, 14)
MESH = pl.DeviceIdType.MESH
D = 1280
WIDTH = HEADS * HEAD_DIM
PAIR = 2 * HEAD_DIM
GROUP = HEADS // 2
ROWS = 128
BLOCK = 256
SEQ = SPAN * ROWS
N_X, N_Z, QUAD = 4, 8, 4
PIECE = GROUP * PAIR
X_ROWS = 160
HALF = X_ROWS // 2
Z_ROWS = 40
Z_PAD = 48
OUT_ROWS = 10
OUT_PAD = 16
NORM_ROWS = 24
TILES = D // 128
BF, F32 = jnp.bfloat16, jnp.float32


def layer_kernel(
    stem_hbm, gain_ref, bias_ref, w_hbm, q_hbm, k_hbm, v_hbm, go_hbm, frames_ref,
    stem_out, out_ref, norm_out,
    stem_ref, w_out, w_qkv, q_ref, k_ref, v_ref, go_ref,
    kv_out, qd_out, kv_in, qd_in, ret_qo, ret_kv, masked_k, kv_t, total,
    xhat, slope, deviation, left_out, left_in, cols, tok_in,
    wide, sends, first, joined, alone, joint_out, z_out, z_in, last_out, last_in,
    norm_a, norm_b, norm_c, norm_mid,
    s_load, s_kv, s_qd, s_qo, s_dkv, s_left, s_pair, s_tok, s_first, s_joined, s_alone, s_z, s_last,
    s_na, s_nb, s_nc,
    r_kv, r_qd, r_cols, r_left, r_pair, r_tok, r_first, r_joined, r_alone, r_z, r_last, r_na, r_nb, r_nc,
):
    me = lax.axis_index("tm")
    side = lax.axis_index("batch")
    slot = lax.rem(me, SPAN)
    base = me - slot
    core = lax.rem(me, 2)
    low = lax.rem(me // 2, 2)
    t = lax.rem(me, QUAD)
    z = lax.rem(me // QUAD, N_Z)
    x = me // (QUAD * N_Z)
    mine8 = side * QUAD + t

    loads = {}
    for index, (name, src, dst) in enumerate(
        (
            ("k", k_hbm.at[0], k_ref), ("v", v_hbm.at[0], v_ref), ("q", q_hbm.at[0], q_ref), ("go", go_hbm.at[0], go_ref),
            ("w_out", w_hbm.at[:, pl.ds(3 * WIDTH, WIDTH)], w_out), ("stem", stem_hbm.at[0], stem_ref),
            ("w_qkv", w_hbm.at[:, pl.ds(0, 3 * WIDTH)], w_qkv),
        )
    ):
        loads[name] = pltpu.make_async_copy(src, dst, s_load.at[index])
        loads[name].start()

    def at_x(step):
        return {"tm": lax.rem(x + step, N_X) * (QUAD * N_Z) + z * QUAD + t}

    def at_z(place):
        return {"tm": x * (QUAD * N_Z) + place * QUAD + t}

    def at_quad(place):
        return {"tm": x * (QUAD * N_Z) + z * QUAD + place}

    def at_eight(step):
        place = lax.rem(mine8 + step, 2 * QUAD)
        return {"tm": x * (QUAD * N_Z) + z * QUAD + lax.rem(place, QUAD), "batch": place // QUAD}

    def remote(src, dst, send_sem, recv_sem, device):
        return pltpu.make_async_remote_copy(
            src_ref=src, dst_ref=dst, send_sem=send_sem, recv_sem=recv_sem,
            device_id=device, device_id_type=MESH,
        )

    def landed(buf, sem):
        pltpu.make_async_copy(buf, buf, sem).wait()

    barrier = pltpu.get_barrier_semaphore()

    def greet(device):
        pl.semaphore_signal(barrier, inc=1, device_id=device, device_id_type=MESH)

    for step in range(1, SPAN):
        greet({"tm": base + lax.rem(slot + step, SPAN)})
    for step in range(1, N_X):
        greet(at_x(step))
    for place in range(QUAD):
        greet(at_z((1 - z // QUAD) * QUAD + place))
    for place in range(QUAD):
        greet({"tm": x * (QUAD * N_Z) + z * QUAD + place, "batch": 1 - side})

    pending = []

    def go(copy):
        copy.start()
        pending.append(copy)

    def go_or_copy(here, copy, src, dst, recv_sem, keep=True):
        pl.when(jnp.logical_not(here))(copy.start)
        pl.when(here)(pltpu.make_async_copy(src, dst, recv_sem).start)
        if keep:
            pending.append((here, copy))

    loads["k"].wait()
    loads["v"].wait()
    for h in range(HEADS):
        at = slice(h * HEAD_DIM, (h + 1) * HEAD_DIM)
        kv_out[h] = jnp.concatenate([k_ref[:, at], v_ref[:, at]], axis=1)
    pl.semaphore_wait(barrier, SPAN - 1 + N_X - 1 + 2 * QUAD)
    for h in range(HEADS):
        copy = remote(kv_out.at[h], kv_in.at[slot], s_kv.at[h], r_kv, {"tm": base + OWNERS[h]})
        go_or_copy(slot == OWNERS[h], copy, kv_out.at[h], kv_in.at[slot], r_kv)
    loads["q"].wait()
    loads["go"].wait()
    loads["w_out"].wait()
    grad_heads = jnp.dot(go_ref[...], w_out[...], preferred_element_type=F32).astype(BF)
    for h in range(HEADS):
        at = slice(h * HEAD_DIM, (h + 1) * HEAD_DIM)
        qd_out[h] = jnp.concatenate([q_ref[:, at], grad_heads[:, at]], axis=1)
    for h in range(HEADS):
        arrival = r_qd.at[slot // 2]
        copy = remote(qd_out.at[h], qd_in.at[slot], s_qd.at[h], arrival, {"tm": base + OWNERS[h]})
        go_or_copy(slot == OWNERS[h], copy, qd_out.at[h], qd_in.at[slot], arrival)

    loads["stem"].wait()
    stem_in = stem_ref[...].astype(F32)
    normal_cdf = 0.5 * (1.0 + lax.erf(stem_in / math.sqrt(2.0)))
    density = jnp.exp(-0.5 * stem_in * stem_in) / math.sqrt(2.0 * math.pi)
    slope[...] = normal_cdf + stem_in * density
    activated = stem_in * normal_cdf
    position = (slot * ROWS + lax.broadcasted_iota(jnp.int32, (ROWS, D // 2), 0)).astype(F32)
    feature = lax.broadcasted_iota(jnp.int32, (ROWS, D // 2), 1).astype(F32)
    angle = position * jnp.exp(-math.log(10000.0) / (D // 2 - 1) * feature)
    embedded = activated + jnp.concatenate([jnp.sin(angle), jnp.cos(angle)], axis=1)
    centered = embedded - jnp.mean(embedded, axis=1, keepdims=True)
    inverse = lax.rsqrt(jnp.mean(centered * centered, axis=1, keepdims=True) + EPSILON)
    standard = centered * inverse
    xhat[...] = standard
    deviation[...] = inverse
    normed = (standard * gain_ref[...] + bias_ref[...]).astype(BF)
    for kind, source in enumerate((normed, go_ref[...])):
        for r in range(2):
            left_out[r, kind] = jnp.concatenate(
                [source[:, c * 2 * X_ROWS + r * X_ROWS : c * 2 * X_ROWS + (r + 1) * X_ROWS] for c in range(N_X)], axis=1
            )
    for place in range(QUAD):
        copy = remote(left_out.at[place % 2], left_in.at[t], s_left.at[place], r_left, at_quad(place))
        go_or_copy(t == place, copy, left_out.at[place % 2], left_in.at[t], r_left)

    head = jnp.int32(0)
    active = jnp.bool_(False)
    for h in range(HEADS):
        head = jnp.where(slot == OWNERS[h], h % GROUP, head)
        active = jnp.logical_or(active, slot == OWNERS[h])
    blocks = SEQ // BLOCK

    def back(buf, index, part, send_sem):
        place = QUAD * (index // 2) + 2 * low + lax.rem(index, 2)
        half = lax.rem(index, 2)
        return place, half, remote(
            buf.at[index], cols.at[part, half, head], send_sem.at[index], r_cols.at[part], {"tm": base + place}
        )

    def send_back(buf, index, part, send_sem):
        place, half, copy = back(buf, index, part, send_sem)
        go_or_copy(slot == place, copy, buf.at[index], cols.at[part, half, head], r_cols.at[part], keep=False)

    @pl.when(active)
    def _():
        limit = frames_ref[0, me // SPAN]
        landed(kv_in, r_kv)
        kv = kv_in[...].reshape(SEQ, PAIR)
        lane = lax.broadcasted_iota(jnp.int32, kv.shape, 1)
        row = lax.broadcasted_iota(jnp.int32, kv.shape, 0)
        fill = jnp.where(jnp.logical_and(lane == HEAD_DIM, 2 * row >= limit), NEG_FILL, 0.0)
        masked_k[...] = jnp.where(lane < HEAD_DIM, kv.astype(F32), fill).astype(BF)
        kv_t[...] = kv.T
        total[...] = jnp.zeros_like(total)
        scale = 1.0 / math.sqrt(HEAD_DIM)
        blane = lax.broadcasted_iota(jnp.int32, (BLOCK, PAIR), 1)
        brow = lax.broadcasted_iota(jnp.int32, (PAIR, BLOCK), 0)
        own = slot // QUAD

        def body(i, carry):
            step = i // 2
            near = lax.rem(own + step, 2) + 2 * lax.rem(own // 2 + step // 2, 2)
            at = 2 * near + lax.rem(i, 2)
            landed(qd_in.at[pl.ds(2 * at, 2)], r_qd.at[at])
            qd = qd_in[pl.ds(2 * at, 2)].reshape(BLOCK, PAIR).astype(F32)
            q_ones = jnp.where(blane < HEAD_DIM, qd * scale, jnp.where(blane == HEAD_DIM, 1.0, 0.0)).astype(BF)
            q_only = jnp.where(blane < HEAD_DIM, qd, 0.0).astype(BF)
            d_only = jnp.where(blane >= HEAD_DIM, qd, 0.0).astype(BF)
            scores = lax.dot_general(masked_k[...], q_ones, (((1,), (1,)), ((), ())), preferred_element_type=F32)
            top = jnp.max(scores, axis=0, keepdims=True)
            power = jnp.exp(scores - top)
            prob = power * (1.0 / jnp.sum(power, axis=0, keepdims=True))
            prob_b = prob.astype(BF)
            attn_t = jnp.dot(kv_t[...], prob_b, preferred_element_type=F32).astype(BF).astype(F32)
            delta = jnp.sum(jnp.where(brow >= HEAD_DIM, qd.T * attn_t, 0.0), axis=0, keepdims=True)
            grad_prob = lax.dot_general(
                kv_in[...].reshape(SEQ, PAIR), d_only, (((1,), (1,)), ((), ())), preferred_element_type=F32
            )
            dscore = (prob * (grad_prob - delta) * scale).astype(BF)
            dq_t = jnp.dot(kv_t[...], dscore, preferred_element_type=F32)
            ret_qo[at] = jnp.where(brow < HEAD_DIM, dq_t, attn_t).T.astype(BF)
            send_back(ret_qo, at, 0, s_qo)
            total[...] += jnp.dot(dscore, q_only, preferred_element_type=F32) + jnp.dot(
                prob_b, d_only, preferred_element_type=F32
            )
            return carry

        lax.fori_loop(0, blocks, body, 0)
        ret_kv[...] = total[...].astype(BF).reshape(blocks, BLOCK, PAIR)

        def send_kv_grads(i, carry):
            send_back(ret_kv, i, 1, s_dkv)
            return carry

        lax.fori_loop(0, blocks, send_kv_grads, 0)

    def spread(part):
        landed(cols.at[part, core], r_cols.at[part])
        go(remote(cols.at[part, core], cols.at[part, core], s_pair.at[part], r_pair.at[part], at_quad(2 * low + 1 - core)))
        for k in range(2):
            copy = remote(
                cols.at[part, core, :, pl.ds(k * ROWS, ROWS)], tok_in.at[part], s_tok.at[part, k], r_tok.at[part],
                at_quad(2 * core + k),
            )
            pl.when(core != low)(copy.start)
            pending.append((core == low, copy))

    tokens = QUAD * ROWS

    def rows_of(step, half):
        chunk = lax.rem(x + step, N_X)
        return pl.ds(pl.multiple_of(chunk * X_ROWS + half * HALF, 16), HALF)

    def multiply(part):
        landed(cols.at[part, 1 - core], r_pair.at[part])
        right = jnp.concatenate([cols[part, :, h].reshape(tokens, PAIR) for h in range(GROUP)], axis=1)
        even = lax.rem(lax.broadcasted_iota(jnp.int32, (128, PIECE), 1), PAIR) < HEAD_DIM
        for at in range(0, PIECE, 128):
            product = lax.dot_general(
                left_in[:, 0, :, at : at + 128].reshape(tokens, 128), right, (((0,), (0,)), ((), ())),
                preferred_element_type=F32,
            )
            if part == 0:
                other = lax.dot_general(
                    left_in[:, 1, :, at : at + 128].reshape(tokens, 128), right, (((0,), (0,)), ((), ())),
                    preferred_element_type=F32,
                )
                product = jnp.where(even, product, other)
            wide[part, at : at + 128] = product
            sends[part, at : at + 128] = product.astype(BF)

    turns = ((0, 1), (1, N_X - 1))

    def ring_start(part):
        for half, step in turns:
            go(remote(sends.at[part, rows_of(2, half)], first.at[part, half], s_first.at[part, half], r_first.at[part, half], at_x(step)))
        for half, step in turns:
            go(remote(sends.at[part, rows_of(step, 1 - half)], alone.at[part, 1 - half], s_alone.at[part, half], r_alone.at[part, 1 - half], at_x(step)))

    def ring_join(part):
        for half, step in turns:
            landed(first.at[part, half], r_first.at[part, half])
            joint_out[part, half] = (first[part, half].astype(F32) + wide[part, rows_of(step, half)]).astype(BF)
            go(remote(joint_out.at[part, half], joined.at[part, half], s_joined.at[part, half], r_joined.at[part, half], at_x(step)))

    def along_z(part):
        for half in range(2):
            landed(alone.at[part, half], r_alone.at[part, half])
            landed(joined.at[part, half], r_joined.at[part, half])
            summed = wide[part, rows_of(0, half)] + alone[part, half].astype(F32) + joined[part, half].astype(F32)
            for k in range(HALF // Z_ROWS):
                z_out[part, half * (HALF // Z_ROWS) + k] = jnp.concatenate(
                    [summed[k * Z_ROWS : (k + 1) * Z_ROWS], jnp.zeros((Z_PAD - Z_ROWS, PIECE), F32)], axis=0
                ).astype(BF)
        for k in range(QUAD):
            place = core * QUAD + k
            copy = remote(z_out.at[part, k], z_in.at[part, z], s_z.at[part, k], r_z.at[part], at_z(place))
            go_or_copy(place == z, copy, z_out.at[part, k], z_in.at[part, z], r_z.at[part])

    spread(0)
    landed(left_in, r_left)
    multiply(0)
    ring_start(0)
    spread(1)
    ring_join(0)
    multiply(1)
    ring_start(1)
    along_z(0)
    ring_join(1)

    loads["w_qkv"].wait()
    landed(tok_in.at[0], r_tok.at[0])
    landed(tok_in.at[1], r_tok.at[1])
    mine = pl.ds(pl.multiple_of(core * ROWS, ROWS), ROWS)

    def tile_of(part, h):
        here = cols[part, low, h % GROUP, mine]
        return jnp.where(low == h // GROUP, here, tok_in[part, h % GROUP])

    qo = [tile_of(0, h) for h in range(HEADS)]
    kv_grads = [tile_of(1, h) for h in range(HEADS)]
    grad_qkv = jnp.concatenate(
        [tile[:, :HEAD_DIM] for tile in qo]
        + [tile[:, :HEAD_DIM] for tile in kv_grads]
        + [tile[:, HEAD_DIM:] for tile in kv_grads],
        axis=1,
    )
    grad_normed = lax.dot_general(grad_qkv, w_qkv[...], (((1,), (1,)), ((), ())), preferred_element_type=F32)
    standard = xhat[...]
    for row, terms in enumerate((jnp.sum(grad_normed * standard, axis=0, keepdims=True), jnp.sum(grad_normed, axis=0, keepdims=True))):
        for k in range(TILES):
            norm_mid[0, row * TILES + k : row * TILES + k + 1] = terms[:, k * 128 : (k + 1) * 128]
    norm_mid[0, 2 * TILES :] = jnp.zeros((NORM_ROWS - 2 * TILES, 128), F32)
    for step in range(1, N_Z):
        go(remote(norm_mid.at[0], norm_a.at[z], s_na.at[step], r_na, at_z(lax.rem(z + step, N_Z))))
    norm_a[z] = norm_mid[0]
    along_z(1)
    gx = grad_normed * gain_ref[...]
    grad_x = go_ref[...].astype(F32) + deviation[...] * (
        gx - jnp.mean(gx, axis=1, keepdims=True) - standard * jnp.mean(gx * standard, axis=1, keepdims=True)
    )
    stem_out[0] = (grad_x * slope[...]).astype(BF)

    landed(norm_a.at[pl.ds(0, N_Z - 1)], r_na)
    norm_mid[1] = jnp.sum(norm_a[...], axis=0)
    for step in range(1, N_X):
        go(remote(norm_mid.at[1], norm_b.at[x], s_nb.at[step], r_nb, at_x(step)))
    norm_b[x] = norm_mid[1]
    landed(norm_b.at[pl.ds(0, N_X - 1)], r_nb)
    norm_mid[2] = jnp.sum(norm_b[...], axis=0)
    for step in range(1, 2 * QUAD):
        go(remote(norm_mid.at[2], norm_c.at[mine8], s_nc.at[step], r_nc, at_eight(step)))
    norm_c[mine8] = norm_mid[2]

    holder = core == z // QUAD
    source = side * 2 + low

    def last_copy(step):
        place = lax.rem(lax.rem(mine8 + step, 2 * QUAD), QUAD)
        return remote(last_out.at[place], last_in.at[source], s_last.at[step], r_last, at_eight(step))

    @pl.when(holder)
    def _():
        for part in range(2):
            landed(z_in.at[part], r_z.at[part])
            summed = jnp.sum(z_in[part].astype(F32), axis=0)
            for place in range(QUAD):
                last_out[place, part] = jnp.concatenate(
                    [summed[place * OUT_ROWS : (place + 1) * OUT_ROWS], jnp.zeros((OUT_PAD - OUT_ROWS, PIECE), F32)], axis=0
                )
        for step in range(1, 2 * QUAD):
            last_copy(step).start()
        pltpu.make_async_copy(last_out.at[t], last_in.at[source], r_last).start()

    landed(norm_c.at[pl.ds(0, 2 * QUAD - 1)], r_nc)
    norms = jnp.sum(norm_c[...], axis=0)
    for row in range(2):
        for k in range(TILES):
            norm_out[row : row + 1, k * 128 : (k + 1) * 128] = norms[row * TILES + k : row * TILES + k + 1]

    landed(last_in, r_last)
    quarters = [[], [], [], []]
    for g in range(2):
        both = last_in[g] + last_in[2 + g]
        for h in range(GROUP):
            for part, (a, b) in enumerate(((0, 3), (1, 2))):
                tile = both[part, :OUT_ROWS, h * PAIR : (h + 1) * PAIR]
                quarters[a].append(tile[:, :HEAD_DIM])
                quarters[b].append(tile[:, HEAD_DIM:])
    for k in range(4):
        out_ref[:, k * WIDTH : (k + 1) * WIDTH] = jnp.concatenate(quarters[k], axis=1)

    for entry in pending:
        if isinstance(entry, tuple):
            pl.when(jnp.logical_not(entry[0]))(entry[1].wait_send)
        else:
            entry.wait_send()

    @pl.when(holder)
    def _():
        for step in range(1, 2 * QUAD):
            last_copy(step).wait_send()

    @pl.when(active)
    def _():
        def drain(i, carry):
            for buf, part, sem in ((ret_qo, 0, s_qo), (ret_kv, 1, s_dkv)):
                place, half, copy = back(buf, i, part, sem)
                pl.when(slot != place)(copy.wait_send)
            return carry

        lax.fori_loop(0, blocks, drain, 0)


def local(stem_pre, gain, bias, w_attn, queries, keys, values, grad_out, frames):
    vmem, dma = pltpu.VMEM, pltpu.SemaphoreType.DMA
    tile = (ROWS, PAIR)
    blocks = SEQ // BLOCK
    anywhere, inside = pl.BlockSpec(memory_space=pl.ANY), pl.BlockSpec(memory_space=vmem)
    return pl.pallas_call(
        layer_kernel,
        out_shape=(
            jax.ShapeDtypeStruct((1, ROWS, D), BF),
            jax.ShapeDtypeStruct((OUT_ROWS, 4 * WIDTH), F32),
            jax.ShapeDtypeStruct((2, D), F32),
        ),
        in_specs=[anywhere, inside, inside, anywhere, anywhere, anywhere, anywhere, anywhere, pl.BlockSpec(memory_space=pltpu.SMEM)],
        out_specs=(inside, inside, inside),
        scratch_shapes=[
            vmem((ROWS, D), BF), vmem((D, WIDTH), BF), vmem((D, 3 * WIDTH), BF),
            vmem((ROWS, WIDTH), BF), vmem((ROWS, WIDTH), BF), vmem((ROWS, WIDTH), BF), vmem((ROWS, D), BF),
            vmem((HEADS,) + tile, BF), vmem((HEADS,) + tile, BF), vmem((SPAN,) + tile, BF), vmem((SPAN,) + tile, BF),
            vmem((blocks, BLOCK, PAIR), BF), vmem((blocks, BLOCK, PAIR), BF),
            vmem((SEQ, PAIR), BF), vmem((PAIR, SEQ), BF), vmem((SEQ, PAIR), F32),
            vmem((ROWS, D), F32), vmem((ROWS, D), F32), vmem((ROWS, 1), F32),
            vmem((2, 2, ROWS, D // 2), BF), vmem((QUAD, 2, ROWS, D // 2), BF),
            vmem((2, 2, GROUP, BLOCK, PAIR), BF), vmem((2, GROUP) + tile, BF),
            vmem((2, D // 2, PIECE), F32), vmem((2, D // 2, PIECE), BF),
            vmem((2, 2, HALF, PIECE), BF), vmem((2, 2, HALF, PIECE), BF), vmem((2, 2, HALF, PIECE), BF), vmem((2, 2, HALF, PIECE), BF),
            vmem((2, QUAD, Z_PAD, PIECE), BF), vmem((2, N_Z, Z_PAD, PIECE), BF),
            vmem((QUAD, 2, OUT_PAD, PIECE), F32), vmem((QUAD, 2, OUT_PAD, PIECE), F32),
            vmem((N_Z, NORM_ROWS, 128), F32), vmem((N_X, NORM_ROWS, 128), F32), vmem((2 * QUAD, NORM_ROWS, 128), F32),
            vmem((3, NORM_ROWS, 128), F32),
            dma((7,)), dma((HEADS,)), dma((HEADS,)), dma((blocks,)), dma((blocks,)), dma((QUAD,)), dma((2,)), dma((2, 2)),
            dma((2, 2)), dma((2, 2)), dma((2, 2)), dma((2, QUAD)), dma((2 * QUAD,)), dma((N_Z,)), dma((N_X,)), dma((2 * QUAD,)),
            dma, dma((blocks,)), dma((2,)), dma, dma((2,)), dma((2,)),
            dma((2, 2)), dma((2, 2)), dma((2, 2)), dma((2,)), dma, dma, dma, dma,
        ],
        compiler_params=pltpu.CompilerParams(
            collective_id=0, has_side_effects=True, vmem_limit_bytes=60 * 1024 * 1024
        ),
        name="layer_backward",
    )(stem_pre, gain.reshape(1, D), bias.reshape(1, D), w_attn, queries, keys, values, grad_out, frames)


def solution(mesh):
    placed = (
        P("batch", "tm", None),
        P(),
        P(),
        P(),
        P("batch", "tm", None),
        P("batch", "tm", None),
        P("batch", "tm", None),
        P("batch", "tm", None),
        P("batch", None),
    )
    return jax.shard_map(
        local,
        mesh=mesh,
        in_specs=placed,
        out_specs=(P("batch", "tm", None), P("tm", None), P()),
        check_vma=False,
    )
```

```python
import math

import jax
import jax.numpy as jnp
from jax import lax
from jax.experimental import pallas as pl
from jax.experimental.pallas import tpu as pltpu
from jax.sharding import PartitionSpec as P

HEAD_DIM = 64
HEADS = 10
SPAN = 16
NEG_FILL = -1e30
EPSILON = 1e-05

OWNERS = (0, 4, 5, 8, 12, 2, 6, 10, 11, 14)
MESH = pl.DeviceIdType.MESH
D = 1280
WIDTH = HEADS * HEAD_DIM
PAIR = 2 * HEAD_DIM
GROUP = HEADS // 2
ROWS = 128
BLOCK = 256
SEQ = SPAN * ROWS
N_X, N_Z, QUAD = 4, 8, 4
PIECE = GROUP * PAIR
X_ROWS = 160
HALF = X_ROWS // 2
Z_ROWS = 40
Z_PAD = 48
OUT_ROWS = 10
OUT_PAD = 16
NORM_ROWS = 24
TILES = D // 128
BF, F32 = jnp.bfloat16, jnp.float32


def layer_kernel(
    stem_hbm, gain_ref, bias_ref, w_hbm, q_hbm, k_hbm, v_hbm, go_hbm, frames_ref,
    stem_hbm_out, out_ref, norm_out,
    stem_ref, w_out, w_qkv, q_ref, k_ref, v_ref, go_ref,
    kv_out, qd_out, kv_in, qd_in, ret_qo, ret_kv, masked_k, kv_t, total,
    xhat, slope, deviation, left_out, left_in, cols, tok_in,
    wide, sends, first, joined, alone, joint_out, z_out, z_in, last_out, last_in,
    norm_a, norm_b, norm_c, norm_mid, stem_out,
    s_load, s_kv, s_qd, s_qo, s_dkv, s_left, s_pair, s_tok, s_first, s_joined, s_alone, s_z, s_last,
    s_na, s_nb, s_nc,
    r_kv, r_qd, r_cols, r_left, r_pair, r_tok, r_first, r_joined, r_alone, r_z, r_last, r_na, r_nb, r_nc,
):
    me = lax.axis_index("tm")
    side = lax.axis_index("batch")
    slot = lax.rem(me, SPAN)
    base = me - slot
    core = lax.rem(me, 2)
    low = lax.rem(me // 2, 2)
    t = lax.rem(me, QUAD)
    z = lax.rem(me // QUAD, N_Z)
    x = me // (QUAD * N_Z)
    mine8 = side * QUAD + t

    loads = {}
    for index, (name, src, dst) in enumerate(
        (
            ("k", k_hbm.at[0], k_ref), ("v", v_hbm.at[0], v_ref), ("q", q_hbm.at[0], q_ref), ("go", go_hbm.at[0], go_ref),
            ("w_out", w_hbm.at[:, pl.ds(3 * WIDTH, WIDTH)], w_out), ("stem", stem_hbm.at[0], stem_ref),
            ("w_qkv", w_hbm.at[:, pl.ds(0, 3 * WIDTH)], w_qkv),
        )
    ):
        loads[name] = pltpu.make_async_copy(src, dst, s_load.at[index])
        loads[name].start()

    def at_x(step):
        return {"tm": lax.rem(x + step, N_X) * (QUAD * N_Z) + z * QUAD + t}

    def at_z(place):
        return {"tm": x * (QUAD * N_Z) + place * QUAD + t}

    def at_quad(place):
        return {"tm": x * (QUAD * N_Z) + z * QUAD + place}

    def at_eight(step):
        place = lax.rem(mine8 + step, 2 * QUAD)
        return {"tm": x * (QUAD * N_Z) + z * QUAD + lax.rem(place, QUAD), "batch": place // QUAD}

    def remote(src, dst, send_sem, recv_sem, device):
        return pltpu.make_async_remote_copy(
            src_ref=src, dst_ref=dst, send_sem=send_sem, recv_sem=recv_sem,
            device_id=device, device_id_type=MESH,
        )

    def landed(buf, sem):
        pltpu.make_async_copy(buf, buf, sem).wait()

    barrier = pltpu.get_barrier_semaphore()

    def greet(device):
        pl.semaphore_signal(barrier, inc=1, device_id=device, device_id_type=MESH)

    for step in range(1, SPAN):
        greet({"tm": base + lax.rem(slot + step, SPAN)})
    for step in range(1, N_X):
        greet(at_x(step))
    for place in range(QUAD):
        greet(at_z((1 - z // QUAD) * QUAD + place))
    for place in range(QUAD):
        greet({"tm": x * (QUAD * N_Z) + z * QUAD + place, "batch": 1 - side})

    pending = []

    def go(copy):
        copy.start()
        pending.append(copy)

    def go_or_copy(here, copy, src, dst, recv_sem, keep=True):
        pl.when(jnp.logical_not(here))(copy.start)
        pl.when(here)(pltpu.make_async_copy(src, dst, recv_sem).start)
        if keep:
            pending.append((here, copy))

    loads["k"].wait()
    loads["v"].wait()
    for h in range(HEADS):
        at = slice(h * HEAD_DIM, (h + 1) * HEAD_DIM)
        kv_out[h] = jnp.concatenate([k_ref[:, at], v_ref[:, at]], axis=1)
    pl.semaphore_wait(barrier, SPAN - 1 + N_X - 1 + 2 * QUAD)
    for h in range(HEADS):
        copy = remote(kv_out.at[h], kv_in.at[slot], s_kv.at[h], r_kv, {"tm": base + OWNERS[h]})
        go_or_copy(slot == OWNERS[h], copy, kv_out.at[h], kv_in.at[slot], r_kv)
    loads["q"].wait()
    loads["go"].wait()
    loads["w_out"].wait()
    grad_heads = jnp.dot(go_ref[...], w_out[...], preferred_element_type=F32).astype(BF)
    for h in range(HEADS):
        at = slice(h * HEAD_DIM, (h + 1) * HEAD_DIM)
        qd_out[h] = jnp.concatenate([q_ref[:, at], grad_heads[:, at]], axis=1)
    for h in range(HEADS):
        arrival = r_qd.at[slot // 2]
        copy = remote(qd_out.at[h], qd_in.at[slot], s_qd.at[h], arrival, {"tm": base + OWNERS[h]})
        go_or_copy(slot == OWNERS[h], copy, qd_out.at[h], qd_in.at[slot], arrival)

    loads["stem"].wait()
    stem_in = stem_ref[...].astype(F32)
    normal_cdf = 0.5 * (1.0 + lax.erf(stem_in / math.sqrt(2.0)))
    density = jnp.exp(-0.5 * stem_in * stem_in) / math.sqrt(2.0 * math.pi)
    slope[...] = normal_cdf + stem_in * density
    activated = stem_in * normal_cdf
    position = (slot * ROWS + lax.broadcasted_iota(jnp.int32, (ROWS, D // 2), 0)).astype(F32)
    feature = lax.broadcasted_iota(jnp.int32, (ROWS, D // 2), 1).astype(F32)
    angle = position * jnp.exp(-math.log(10000.0) / (D // 2 - 1) * feature)
    embedded = activated + jnp.concatenate([jnp.sin(angle), jnp.cos(angle)], axis=1)
    centered = embedded - jnp.mean(embedded, axis=1, keepdims=True)
    inverse = lax.rsqrt(jnp.mean(centered * centered, axis=1, keepdims=True) + EPSILON)
    standard = centered * inverse
    xhat[...] = standard
    deviation[...] = inverse
    normed = (standard * gain_ref[...].reshape(1, D) + bias_ref[...].reshape(1, D)).astype(BF)
    for kind, source in enumerate((normed, go_ref[...])):
        for r in range(2):
            left_out[r, kind] = jnp.concatenate(
                [source[:, c * 2 * X_ROWS + r * X_ROWS : c * 2 * X_ROWS + (r + 1) * X_ROWS] for c in range(N_X)], axis=1
            )
    for place in range(QUAD):
        copy = remote(left_out.at[place % 2], left_in.at[t], s_left.at[place], r_left, at_quad(place))
        go_or_copy(t == place, copy, left_out.at[place % 2], left_in.at[t], r_left)

    head = jnp.int32(0)
    active = jnp.bool_(False)
    for h in range(HEADS):
        head = jnp.where(slot == OWNERS[h], h % GROUP, head)
        active = jnp.logical_or(active, slot == OWNERS[h])
    blocks = SEQ // BLOCK

    def back(buf, index, part, send_sem):
        place = QUAD * (index // 2) + 2 * low + lax.rem(index, 2)
        half = lax.rem(index, 2)
        return place, half, remote(
            buf.at[index], cols.at[part, half, head], send_sem.at[index], r_cols.at[part], {"tm": base + place}
        )

    def send_back(buf, index, part, send_sem):
        place, half, copy = back(buf, index, part, send_sem)
        go_or_copy(slot == place, copy, buf.at[index], cols.at[part, half, head], r_cols.at[part], keep=False)

    @pl.when(active)
    def _():
        limit = frames_ref[0, me // SPAN]
        landed(kv_in, r_kv)
        kv = kv_in[...].reshape(SEQ, PAIR)
        lane = lax.broadcasted_iota(jnp.int32, kv.shape, 1)
        row = lax.broadcasted_iota(jnp.int32, kv.shape, 0)
        fill = jnp.where(jnp.logical_and(lane == HEAD_DIM, 2 * row >= limit), NEG_FILL, 0.0)
        masked_k[...] = jnp.where(lane < HEAD_DIM, kv.astype(F32), fill).astype(BF)
        kv_t[...] = kv.T
        total[...] = jnp.zeros_like(total)
        scale = 1.0 / math.sqrt(HEAD_DIM)
        blane = lax.broadcasted_iota(jnp.int32, (BLOCK, PAIR), 1)
        brow = lax.broadcasted_iota(jnp.int32, (PAIR, BLOCK), 0)
        own = slot // QUAD

        def body(i, carry):
            step = i // 2
            near = lax.rem(own + step, 2) + 2 * lax.rem(own // 2 + step // 2, 2)
            at = 2 * near + lax.rem(i, 2)
            landed(qd_in.at[pl.ds(2 * at, 2)], r_qd.at[at])
            qd = qd_in[pl.ds(2 * at, 2)].reshape(BLOCK, PAIR).astype(F32)
            q_ones = jnp.where(blane < HEAD_DIM, qd * scale, jnp.where(blane == HEAD_DIM, 1.0, 0.0)).astype(BF)
            q_only = jnp.where(blane < HEAD_DIM, qd, 0.0).astype(BF)
            d_only = jnp.where(blane >= HEAD_DIM, qd, 0.0).astype(BF)
            scores = lax.dot_general(masked_k[...], q_ones, (((1,), (1,)), ((), ())), preferred_element_type=F32)
            top = jnp.max(scores, axis=0, keepdims=True)
            power = jnp.exp(scores - top)
            prob = power * (1.0 / jnp.sum(power, axis=0, keepdims=True))
            prob_b = prob.astype(BF)
            attn_t = jnp.dot(kv_t[...], prob_b, preferred_element_type=F32).astype(BF).astype(F32)
            delta = jnp.sum(jnp.where(brow >= HEAD_DIM, qd.T * attn_t, 0.0), axis=0, keepdims=True)
            grad_prob = lax.dot_general(
                kv_in[...].reshape(SEQ, PAIR), d_only, (((1,), (1,)), ((), ())), preferred_element_type=F32
            )
            dscore = (prob * (grad_prob - delta) * scale).astype(BF)
            dq_t = jnp.dot(kv_t[...], dscore, preferred_element_type=F32)
            ret_qo[at] = jnp.where(brow < HEAD_DIM, dq_t, attn_t).T.astype(BF)
            send_back(ret_qo, at, 0, s_qo)
            total[...] += jnp.dot(dscore, q_only, preferred_element_type=F32) + jnp.dot(
                prob_b, d_only, preferred_element_type=F32
            )
            return carry

        lax.fori_loop(0, blocks, body, 0)
        ret_kv[...] = total[...].astype(BF).reshape(blocks, BLOCK, PAIR)

        def send_kv_grads(i, carry):
            send_back(ret_kv, i, 1, s_dkv)
            return carry

        lax.fori_loop(0, blocks, send_kv_grads, 0)

    def spread(part):
        landed(cols.at[part, core], r_cols.at[part])
        go(remote(cols.at[part, core], cols.at[part, core], s_pair.at[part], r_pair.at[part], at_quad(2 * low + 1 - core)))
        for k in range(2):
            copy = remote(
                cols.at[part, core, :, pl.ds(k * ROWS, ROWS)], tok_in.at[part], s_tok.at[part, k], r_tok.at[part],
                at_quad(2 * core + k),
            )
            pl.when(core != low)(copy.start)
            pending.append((core == low, copy))

    tokens = QUAD * ROWS

    def rows_of(step, half):
        chunk = lax.rem(x + step, N_X)
        return pl.ds(pl.multiple_of(chunk * X_ROWS + half * HALF, 16), HALF)

    def multiply(part):
        landed(cols.at[part, 1 - core], r_pair.at[part])
        right = jnp.concatenate([cols[part, :, h].reshape(tokens, PAIR) for h in range(GROUP)], axis=1)
        even = lax.rem(lax.broadcasted_iota(jnp.int32, (128, PIECE), 1), PAIR) < HEAD_DIM
        for at in range(0, PIECE, 128):
            product = lax.dot_general(
                left_in[:, 0, :, at : at + 128].reshape(tokens, 128), right, (((0,), (0,)), ((), ())),
                preferred_element_type=F32,
            )
            if part == 0:
                other = lax.dot_general(
                    left_in[:, 1, :, at : at + 128].reshape(tokens, 128), right, (((0,), (0,)), ((), ())),
                    preferred_element_type=F32,
                )
                product = jnp.where(even, product, other)
            wide[part, at : at + 128] = product
            sends[part, at : at + 128] = product.astype(BF)

    turns = ((0, 1), (1, N_X - 1))

    def ring_start(part):
        for half, step in turns:
            go(remote(sends.at[part, rows_of(2, half)], first.at[part, half], s_first.at[part, half], r_first.at[part, half], at_x(step)))
        for half, step in turns:
            go(remote(sends.at[part, rows_of(step, 1 - half)], alone.at[part, 1 - half], s_alone.at[part, half], r_alone.at[part, 1 - half], at_x(step)))

    def ring_join(part):
        for half, step in turns:
            landed(first.at[part, half], r_first.at[part, half])
            joint_out[part, half] = (first[part, half].astype(F32) + wide[part, rows_of(step, half)]).astype(BF)
            go(remote(joint_out.at[part, half], joined.at[part, half], s_joined.at[part, half], r_joined.at[part, half], at_x(step)))

    def along_z(part):
        for half in range(2):
            landed(alone.at[part, half], r_alone.at[part, half])
            landed(joined.at[part, half], r_joined.at[part, half])
            summed = wide[part, rows_of(0, half)] + alone[part, half].astype(F32) + joined[part, half].astype(F32)
            for k in range(HALF // Z_ROWS):
                z_out[part, half * (HALF // Z_ROWS) + k] = jnp.concatenate(
                    [summed[k * Z_ROWS : (k + 1) * Z_ROWS], jnp.zeros((Z_PAD - Z_ROWS, PIECE), F32)], axis=0
                ).astype(BF)
        for k in range(QUAD):
            place = core * QUAD + k
            copy = remote(z_out.at[part, k], z_in.at[part, z], s_z.at[part, k], r_z.at[part], at_z(place))
            go_or_copy(place == z, copy, z_out.at[part, k], z_in.at[part, z], r_z.at[part])

    spread(0)
    landed(left_in, r_left)
    multiply(0)
    ring_start(0)
    spread(1)
    ring_join(0)
    multiply(1)
    ring_start(1)
    along_z(0)
    ring_join(1)

    loads["w_qkv"].wait()
    landed(tok_in.at[0], r_tok.at[0])
    landed(tok_in.at[1], r_tok.at[1])
    mine = pl.ds(pl.multiple_of(core * ROWS, ROWS), ROWS)

    def tile_of(part, h):
        here = cols[part, low, h % GROUP, mine]
        return jnp.where(low == h // GROUP, here, tok_in[part, h % GROUP])

    qo = [tile_of(0, h) for h in range(HEADS)]
    kv_grads = [tile_of(1, h) for h in range(HEADS)]
    grad_qkv = jnp.concatenate(
        [tile[:, :HEAD_DIM] for tile in qo]
        + [tile[:, :HEAD_DIM] for tile in kv_grads]
        + [tile[:, HEAD_DIM:] for tile in kv_grads],
        axis=1,
    )
    grad_normed = lax.dot_general(grad_qkv, w_qkv[...], (((1,), (1,)), ((), ())), preferred_element_type=F32)
    standard = xhat[...]
    for row, terms in enumerate((jnp.sum(grad_normed * standard, axis=0, keepdims=True), jnp.sum(grad_normed, axis=0, keepdims=True))):
        for k in range(TILES):
            norm_mid[0, row * TILES + k : row * TILES + k + 1] = terms[:, k * 128 : (k + 1) * 128]
    norm_mid[0, 2 * TILES :] = jnp.zeros((NORM_ROWS - 2 * TILES, 128), F32)
    for step in range(1, N_Z):
        go(remote(norm_mid.at[0], norm_a.at[z], s_na.at[step], r_na, at_z(lax.rem(z + step, N_Z))))
    norm_a[z] = norm_mid[0]
    along_z(1)
    gx = grad_normed * gain_ref[...].reshape(1, D)
    grad_x = go_ref[...].astype(F32) + deviation[...] * (
        gx - jnp.mean(gx, axis=1, keepdims=True) - standard * jnp.mean(gx * standard, axis=1, keepdims=True)
    )
    stem_out[...] = (grad_x * slope[...]).astype(BF)
    stem_copy = pltpu.make_async_copy(stem_out, stem_hbm_out.at[0], s_load.at[7])
    stem_copy.start()

    landed(norm_a.at[pl.ds(0, N_Z - 1)], r_na)
    norm_mid[1] = jnp.sum(norm_a[...], axis=0)
    for step in range(1, N_X):
        go(remote(norm_mid.at[1], norm_b.at[x], s_nb.at[step], r_nb, at_x(step)))
    norm_b[x] = norm_mid[1]
    landed(norm_b.at[pl.ds(0, N_X - 1)], r_nb)
    norm_mid[2] = jnp.sum(norm_b[...], axis=0)
    for step in range(1, 2 * QUAD):
        go(remote(norm_mid.at[2], norm_c.at[mine8], s_nc.at[step], r_nc, at_eight(step)))
    norm_c[mine8] = norm_mid[2]

    holder = core == z // QUAD
    source = side * 2 + low

    def last_copy(step):
        place = lax.rem(lax.rem(mine8 + step, 2 * QUAD), QUAD)
        return remote(last_out.at[place], last_in.at[source], s_last.at[step], r_last, at_eight(step))

    @pl.when(holder)
    def _():
        for part in range(2):
            landed(z_in.at[part], r_z.at[part])
            summed = jnp.sum(z_in[part].astype(F32), axis=0)
            for place in range(QUAD):
                last_out[place, part] = jnp.concatenate(
                    [summed[place * OUT_ROWS : (place + 1) * OUT_ROWS], jnp.zeros((OUT_PAD - OUT_ROWS, PIECE), F32)], axis=0
                ).astype(BF)
        for step in range(1, 2 * QUAD):
            last_copy(step).start()
        pltpu.make_async_copy(last_out.at[t], last_in.at[source], r_last).start()

    landed(norm_c.at[pl.ds(0, 2 * QUAD - 1)], r_nc)
    norms = jnp.sum(norm_c[...], axis=0)
    for row in range(2):
        for k in range(TILES):
            norm_out[row : row + 1, k * 128 : (k + 1) * 128] = norms[row * TILES + k : row * TILES + k + 1]

    landed(last_in, r_last)
    quarters = [[], [], [], []]
    for g in range(2):
        both = last_in[g].astype(F32) + last_in[2 + g].astype(F32)
        for h in range(GROUP):
            for part, (a, b) in enumerate(((0, 3), (1, 2))):
                tile = both[part, :OUT_ROWS, h * PAIR : (h + 1) * PAIR]
                quarters[a].append(tile[:, :HEAD_DIM])
                quarters[b].append(tile[:, HEAD_DIM:])
    for k in range(4):
        out_ref[:, k * WIDTH : (k + 1) * WIDTH] = jnp.concatenate(quarters[k], axis=1)

    stem_copy.wait()
    for entry in pending:
        if isinstance(entry, tuple):
            pl.when(jnp.logical_not(entry[0]))(entry[1].wait_send)
        else:
            entry.wait_send()

    @pl.when(holder)
    def _():
        for step in range(1, 2 * QUAD):
            last_copy(step).wait_send()

    @pl.when(active)
    def _():
        def drain(i, carry):
            for buf, part, sem in ((ret_qo, 0, s_qo), (ret_kv, 1, s_dkv)):
                place, half, copy = back(buf, i, part, sem)
                pl.when(slot != place)(copy.wait_send)
            return carry

        lax.fori_loop(0, blocks, drain, 0)


def copy_kernel(a, b, c, a_out, b_out, c_out, a_mid, b_mid, c_mid, sems):
    routes = ((a, a_mid, a_out), (b, b_mid, b_out), (c, c_mid, c_out))
    inward = [pltpu.make_async_copy(src, mid, sems.at[0, index]) for index, (src, mid, dst) in enumerate(routes)]
    outward = [pltpu.make_async_copy(mid, dst, sems.at[1, index]) for index, (src, mid, dst) in enumerate(routes)]
    for copy in inward:
        copy.start()
    for first, second in zip(inward, outward):
        first.wait()
        second.start()
    for copy in outward:
        copy.wait()


def hand_on(*arrays):
    anywhere = pl.BlockSpec(memory_space=pl.ANY)
    return pl.pallas_call(
        copy_kernel,
        out_shape=tuple(jax.ShapeDtypeStruct(array.shape, array.dtype) for array in arrays),
        in_specs=[anywhere] * 3,
        out_specs=(anywhere,) * 3,
        scratch_shapes=[pltpu.VMEM(array.shape, array.dtype) for array in arrays] + [pltpu.SemaphoreType.DMA((2, 3))],
        compiler_params=pltpu.CompilerParams(vmem_limit_bytes=63 * 1024 * 1024),
        name="hand_on",
    )(*arrays)


def local(stem_pre, gain, bias, w_attn, queries, keys, values, grad_out, frames):
    vmem, dma = pltpu.VMEM, pltpu.SemaphoreType.DMA
    tile = (ROWS, PAIR)
    blocks = SEQ // BLOCK
    anywhere, inside = pl.BlockSpec(memory_space=pl.ANY), pl.BlockSpec(memory_space=vmem)
    results = pl.pallas_call(
        layer_kernel,
        out_shape=(
            jax.ShapeDtypeStruct((1, ROWS, D), BF),
            jax.ShapeDtypeStruct((OUT_ROWS, 4 * WIDTH), F32),
            jax.ShapeDtypeStruct((2, D), F32),
        ),
        in_specs=[anywhere, inside, inside, anywhere, anywhere, anywhere, anywhere, anywhere, pl.BlockSpec(memory_space=pltpu.SMEM)],
        out_specs=(anywhere, inside, inside),
        scratch_shapes=[
            vmem((ROWS, D), BF), vmem((D, WIDTH), BF), vmem((D, 3 * WIDTH), BF),
            vmem((ROWS, WIDTH), BF), vmem((ROWS, WIDTH), BF), vmem((ROWS, WIDTH), BF), vmem((ROWS, D), BF),
            vmem((HEADS,) + tile, BF), vmem((HEADS,) + tile, BF), vmem((SPAN,) + tile, BF), vmem((SPAN,) + tile, BF),
            vmem((blocks, BLOCK, PAIR), BF), vmem((blocks, BLOCK, PAIR), BF),
            vmem((SEQ, PAIR), BF), vmem((PAIR, SEQ), BF), vmem((SEQ, PAIR), F32),
            vmem((ROWS, D), F32), vmem((ROWS, D), F32), vmem((ROWS, 1), F32),
            vmem((2, 2, ROWS, D // 2), BF), vmem((QUAD, 2, ROWS, D // 2), BF),
            vmem((2, 2, GROUP, BLOCK, PAIR), BF), vmem((2, GROUP) + tile, BF),
            vmem((2, D // 2, PIECE), F32), vmem((2, D // 2, PIECE), BF),
            vmem((2, 2, HALF, PIECE), BF), vmem((2, 2, HALF, PIECE), BF), vmem((2, 2, HALF, PIECE), BF), vmem((2, 2, HALF, PIECE), BF),
            vmem((2, QUAD, Z_PAD, PIECE), BF), vmem((2, N_Z, Z_PAD, PIECE), BF),
            vmem((QUAD, 2, OUT_PAD, PIECE), BF), vmem((QUAD, 2, OUT_PAD, PIECE), BF),
            vmem((N_Z, NORM_ROWS, 128), F32), vmem((N_X, NORM_ROWS, 128), F32), vmem((2 * QUAD, NORM_ROWS, 128), F32),
            vmem((3, NORM_ROWS, 128), F32), vmem((ROWS, D), BF),
            dma((8,)), dma((HEADS,)), dma((HEADS,)), dma((blocks,)), dma((blocks,)), dma((QUAD,)), dma((2,)), dma((2, 2)),
            dma((2, 2)), dma((2, 2)), dma((2, 2)), dma((2, QUAD)), dma((2 * QUAD,)), dma((N_Z,)), dma((N_X,)), dma((2 * QUAD,)),
            dma, dma((blocks,)), dma((2,)), dma, dma((2,)), dma((2,)),
            dma((2, 2)), dma((2, 2)), dma((2, 2)), dma((2,)), dma, dma, dma, dma,
        ],
        compiler_params=pltpu.CompilerParams(
            collective_id=0, has_side_effects=True, vmem_limit_bytes=60 * 1024 * 1024
        ),
        name="layer_backward",
    )(stem_pre, gain, bias, w_attn, queries, keys, values, grad_out, frames)
    return hand_on(*results)


def solution(mesh):
    placed = (
        P("batch", "tm", None),
        P(),
        P(),
        P(),
        P("batch", "tm", None),
        P("batch", "tm", None),
        P("batch", "tm", None),
        P("batch", "tm", None),
        P("batch", None),
    )
    return jax.shard_map(
        local,
        mesh=mesh,
        in_specs=placed,
        out_specs=(P("batch", "tm", None), P("tm", None), P()),
        check_vma=False,
    )
```

```python
import math

import jax
import jax.numpy as jnp
from jax import lax
from jax.experimental import pallas as pl
from jax.experimental.pallas import tpu as pltpu
from jax.sharding import PartitionSpec as P

HEAD_DIM = 64
HEADS = 10
SPAN = 16
NEG_FILL = -1e30
EPSILON = 1e-05

OWNERS = (0, 4, 5, 8, 12, 2, 6, 10, 11, 14)
MESH = pl.DeviceIdType.MESH
D = 1280
WIDTH = HEADS * HEAD_DIM
PAIR = 2 * HEAD_DIM
GROUP = HEADS // 2
ROWS = 128
BLOCK = 256
SEQ = SPAN * ROWS
N_X, N_Z, QUAD = 4, 8, 4
PIECE = GROUP * PAIR
X_ROWS = 160
HALF = X_ROWS // 2
Z_ROWS = 40
Z_PAD = 48
OUT_ROWS = 10
OUT_PAD = 16
NORM_ROWS = 24
TILES = D // 128
CHUNK = 1024
BF, F32 = jnp.bfloat16, jnp.float32


def layer_kernel(
    stem_hbm, gain_ref, bias_ref, w_hbm, q_hbm, k_hbm, v_hbm, go_hbm, frames_ref,
    stem_hbm_out, out_ref, norm_out,
    stem_ref, w_out, w_qkv, q_ref, k_ref, v_ref, go_ref,
    kv_out, qd_out, kv_in, qd_in, ret_qo, ret_kv, masked_k, kv_t, total, scores, powers,
    xhat, slope, deviation, left_out, left_in, cols, tok_in,
    wide, sends, first, joined, alone, joint_out, z_out, z_in, last_out, last_in,
    norm_a, norm_b, norm_c, norm_mid, stem_out,
    s_load, s_kv, s_qd, s_qo, s_dkv, s_left, s_pair, s_tok, s_first, s_joined, s_alone, s_z, s_last,
    s_na, s_nb, s_nc,
    r_kv, r_qd, r_cols, r_left, r_pair, r_tok, r_first, r_joined, r_alone, r_z, r_last, r_na, r_nb, r_nc,
):
    me = lax.axis_index("tm")
    side = lax.axis_index("batch")
    slot = lax.rem(me, SPAN)
    base = me - slot
    core = lax.rem(me, 2)
    low = lax.rem(me // 2, 2)
    t = lax.rem(me, QUAD)
    z = lax.rem(me // QUAD, N_Z)
    x = me // (QUAD * N_Z)
    mine8 = side * QUAD + t

    loads = {}
    for index, (name, src, dst) in enumerate(
        (
            ("k", k_hbm.at[0], k_ref), ("v", v_hbm.at[0], v_ref), ("q", q_hbm.at[0], q_ref), ("go", go_hbm.at[0], go_ref),
            ("w_out", w_hbm.at[:, pl.ds(3 * WIDTH, WIDTH)], w_out), ("stem", stem_hbm.at[0], stem_ref),
            ("w_qkv", w_hbm.at[:, pl.ds(0, 3 * WIDTH)], w_qkv),
        )
    ):
        loads[name] = pltpu.make_async_copy(src, dst, s_load.at[index])
        loads[name].start()

    def at_x(step):
        return {"tm": lax.rem(x + step, N_X) * (QUAD * N_Z) + z * QUAD + t}

    def at_z(place):
        return {"tm": x * (QUAD * N_Z) + place * QUAD + t}

    def at_quad(place):
        return {"tm": x * (QUAD * N_Z) + z * QUAD + place}

    def at_eight(step):
        place = lax.rem(mine8 + step, 2 * QUAD)
        return {"tm": x * (QUAD * N_Z) + z * QUAD + lax.rem(place, QUAD), "batch": place // QUAD}

    def remote(src, dst, send_sem, recv_sem, device):
        return pltpu.make_async_remote_copy(
            src_ref=src, dst_ref=dst, send_sem=send_sem, recv_sem=recv_sem,
            device_id=device, device_id_type=MESH,
        )

    def landed(buf, sem):
        pltpu.make_async_copy(buf, buf, sem).wait()

    barrier = pltpu.get_barrier_semaphore()

    def greet(device):
        pl.semaphore_signal(barrier, inc=1, device_id=device, device_id_type=MESH)

    for step in range(1, SPAN):
        greet({"tm": base + lax.rem(slot + step, SPAN)})
    for step in range(1, N_X):
        greet(at_x(step))
    for place in range(QUAD):
        greet(at_z((1 - z // QUAD) * QUAD + place))
    for place in range(QUAD):
        greet({"tm": x * (QUAD * N_Z) + z * QUAD + place, "batch": 1 - side})

    pending = []

    def go(copy):
        copy.start()
        pending.append(copy)

    def go_or_copy(here, copy, src, dst, recv_sem, keep=True):
        pl.when(jnp.logical_not(here))(copy.start)
        pl.when(here)(pltpu.make_async_copy(src, dst, recv_sem).start)
        if keep:
            pending.append((here, copy))

    loads["k"].wait()
    loads["v"].wait()
    for h in range(HEADS):
        at = slice(h * HEAD_DIM, (h + 1) * HEAD_DIM)
        kv_out[h] = jnp.concatenate([k_ref[:, at], v_ref[:, at]], axis=1)
    pl.semaphore_wait(barrier, SPAN - 1 + N_X - 1 + 2 * QUAD)
    for h in range(HEADS):
        copy = remote(kv_out.at[h], kv_in.at[slot], s_kv.at[h], r_kv, {"tm": base + OWNERS[h]})
        go_or_copy(slot == OWNERS[h], copy, kv_out.at[h], kv_in.at[slot], r_kv)
    loads["q"].wait()
    loads["go"].wait()
    loads["w_out"].wait()
    grad_heads = jnp.dot(go_ref[...], w_out[...], preferred_element_type=F32).astype(BF)
    for h in range(HEADS):
        at = slice(h * HEAD_DIM, (h + 1) * HEAD_DIM)
        qd_out[h] = jnp.concatenate([q_ref[:, at], grad_heads[:, at]], axis=1)
    for h in range(HEADS):
        arrival = r_qd.at[slot // 2]
        copy = remote(qd_out.at[h], qd_in.at[slot], s_qd.at[h], arrival, {"tm": base + OWNERS[h]})
        go_or_copy(slot == OWNERS[h], copy, qd_out.at[h], qd_in.at[slot], arrival)

    loads["stem"].wait()
    stem_in = stem_ref[...].astype(F32)
    normal_cdf = 0.5 * (1.0 + lax.erf(stem_in / math.sqrt(2.0)))
    density = jnp.exp(-0.5 * stem_in * stem_in) / math.sqrt(2.0 * math.pi)
    slope[...] = normal_cdf + stem_in * density
    activated = stem_in * normal_cdf
    position = (slot * ROWS + lax.broadcasted_iota(jnp.int32, (ROWS, D // 2), 0)).astype(F32)
    feature = lax.broadcasted_iota(jnp.int32, (ROWS, D // 2), 1).astype(F32)
    angle = position * jnp.exp(-math.log(10000.0) / (D // 2 - 1) * feature)
    embedded = activated + jnp.concatenate([jnp.sin(angle), jnp.cos(angle)], axis=1)
    centered = embedded - jnp.mean(embedded, axis=1, keepdims=True)
    inverse = lax.rsqrt(jnp.mean(centered * centered, axis=1, keepdims=True) + EPSILON)
    standard = centered * inverse
    xhat[...] = standard
    deviation[...] = inverse
    normed = (standard * gain_ref[...].reshape(1, D) + bias_ref[...].reshape(1, D)).astype(BF)
    for kind, source in enumerate((normed, go_ref[...])):
        for r in range(2):
            left_out[r, kind] = jnp.concatenate(
                [source[:, c * 2 * X_ROWS + r * X_ROWS : c * 2 * X_ROWS + (r + 1) * X_ROWS] for c in range(N_X)], axis=1
            )
    for place in range(QUAD):
        copy = remote(left_out.at[place % 2], left_in.at[t], s_left.at[place], r_left, at_quad(place))
        go_or_copy(t == place, copy, left_out.at[place % 2], left_in.at[t], r_left)

    head = jnp.int32(0)
    active = jnp.bool_(False)
    for h in range(HEADS):
        head = jnp.where(slot == OWNERS[h], h % GROUP, head)
        active = jnp.logical_or(active, slot == OWNERS[h])
    blocks = SEQ // BLOCK

    def back(buf, index, part, send_sem):
        place = QUAD * (index // 2) + 2 * low + lax.rem(index, 2)
        half = lax.rem(index, 2)
        return place, half, remote(
            buf.at[index], cols.at[part, half, head], send_sem.at[index], r_cols.at[part], {"tm": base + place}
        )

    def send_back(buf, index, part, send_sem):
        place, half, copy = back(buf, index, part, send_sem)
        go_or_copy(slot == place, copy, buf.at[index], cols.at[part, half, head], r_cols.at[part], keep=False)

    @pl.when(active)
    def _():
        limit = frames_ref[0, me // SPAN]
        landed(kv_in, r_kv)
        kv = kv_in[...].reshape(SEQ, PAIR)
        lane = lax.broadcasted_iota(jnp.int32, kv.shape, 1)
        row = lax.broadcasted_iota(jnp.int32, kv.shape, 0)
        fill = jnp.where(jnp.logical_and(lane == HEAD_DIM, 2 * row >= limit), NEG_FILL, 0.0)
        masked_k[...] = jnp.where(lane < HEAD_DIM, kv.astype(F32), fill).astype(BF)
        kv_t[...] = kv.T
        total[...] = jnp.zeros_like(total)
        scale = 1.0 / math.sqrt(HEAD_DIM)
        blane = lax.broadcasted_iota(jnp.int32, (BLOCK, PAIR), 1)
        own = slot // QUAD

        def body(i, carry):
            step = i // 2
            near = lax.rem(own + step, 2) + 2 * lax.rem(own // 2 + step // 2, 2)
            at = 2 * near + lax.rem(i, 2)
            landed(qd_in.at[pl.ds(2 * at, 2)], r_qd.at[at])
            qd = qd_in[pl.ds(2 * at, 2)].reshape(BLOCK, PAIR).astype(F32)
            q_ones = jnp.where(blane < HEAD_DIM, qd * scale, jnp.where(blane == HEAD_DIM, 1.0, 0.0)).astype(BF)
            q_only = jnp.where(blane < HEAD_DIM, qd, 0.0).astype(BF)
            top = jnp.full((8, BLOCK), NEG_FILL, F32)
            for c in range(0, SEQ, CHUNK):
                part = lax.dot_general(
                    masked_k[c : c + CHUNK], q_ones, (((1,), (1,)), ((), ())), preferred_element_type=F32
                )
                scores[c : c + CHUNK] = part
                top = jnp.maximum(top, jnp.max(part.reshape(CHUNK // 8, 8, BLOCK), axis=0))
            top = jnp.max(top, axis=0, keepdims=True)
            mass = jnp.zeros((8, BLOCK), F32)
            attn_t = jnp.zeros((HEAD_DIM, BLOCK), F32)
            for c in range(0, SEQ, CHUNK):
                power = jnp.exp(scores[c : c + CHUNK] - top)
                mass = mass + jnp.sum(power.reshape(CHUNK // 8, 8, BLOCK), axis=0)
                power_b = power.astype(BF)
                powers[c : c + CHUNK] = power_b
                attn_t = attn_t + jnp.dot(kv_t[HEAD_DIM:, c : c + CHUNK], power_b, preferred_element_type=F32)
            inverse_mass = 1.0 / jnp.sum(mass, axis=0, keepdims=True)
            attn_t = (attn_t * inverse_mass).astype(BF).astype(F32)
            shared_t = qd.T[HEAD_DIM:] * inverse_mass
            shared = jnp.concatenate([jnp.zeros((HEAD_DIM, BLOCK), F32), shared_t], axis=0).T
            d_only = shared.astype(BF)
            d_scaled = (shared * scale).astype(BF)
            delta = scale * jnp.sum(shared_t.astype(BF).astype(F32) * attn_t, axis=0, keepdims=True)
            dq_t = jnp.zeros((HEAD_DIM, BLOCK), F32)
            for c in range(0, SEQ, CHUNK):
                grad_prob = lax.dot_general(
                    kv_in[c // ROWS : (c + CHUNK) // ROWS].reshape(CHUNK, PAIR), d_scaled, (((1,), (1,)), ((), ())),
                    preferred_element_type=F32,
                )
                power_b = powers[c : c + CHUNK]
                dscore = (power_b.astype(F32) * (grad_prob - delta)).astype(BF)
                dq_t = dq_t + jnp.dot(kv_t[:HEAD_DIM, c : c + CHUNK], dscore, preferred_element_type=F32)
                total[c : c + CHUNK] += jnp.dot(dscore, q_only, preferred_element_type=F32) + jnp.dot(
                    power_b, d_only, preferred_element_type=F32
                )
            ret_qo[at] = jnp.concatenate([dq_t, attn_t], axis=0).T.astype(BF)
            send_back(ret_qo, at, 0, s_qo)
            return carry

        lax.fori_loop(0, blocks, body, 0)
        ret_kv[...] = total[...].astype(BF).reshape(blocks, BLOCK, PAIR)

        def send_kv_grads(i, carry):
            send_back(ret_kv, i, 1, s_dkv)
            return carry

        lax.fori_loop(0, blocks, send_kv_grads, 0)

    def spread(part):
        landed(cols.at[part, core], r_cols.at[part])
        go(remote(cols.at[part, core], cols.at[part, core], s_pair.at[part], r_pair.at[part], at_quad(2 * low + 1 - core)))
        for k in range(2):
            copy = remote(
                cols.at[part, core, :, pl.ds(k * ROWS, ROWS)], tok_in.at[part], s_tok.at[part, k], r_tok.at[part],
                at_quad(2 * core + k),
            )
            pl.when(core != low)(copy.start)
            pending.append((core == low, copy))

    tokens = QUAD * ROWS

    def rows_of(step, half):
        chunk = lax.rem(x + step, N_X)
        return pl.ds(pl.multiple_of(chunk * X_ROWS + half * HALF, 16), HALF)

    def multiply(part):
        landed(cols.at[part, 1 - core], r_pair.at[part])
        right = jnp.concatenate([cols[part, :, h].reshape(tokens, PAIR) for h in range(GROUP)], axis=1)
        even = lax.rem(lax.broadcasted_iota(jnp.int32, (128, PIECE), 1), PAIR) < HEAD_DIM
        for at in range(0, PIECE, 128):
            product = lax.dot_general(
                left_in[:, 0, :, at : at + 128].reshape(tokens, 128), right, (((0,), (0,)), ((), ())),
                preferred_element_type=F32,
            )
            if part == 0:
                other = lax.dot_general(
                    left_in[:, 1, :, at : at + 128].reshape(tokens, 128), right, (((0,), (0,)), ((), ())),
                    preferred_element_type=F32,
                )
                product = jnp.where(even, product, other)
            wide[part, at : at + 128] = product
            sends[part, at : at + 128] = product.astype(BF)

    turns = ((0, 1), (1, N_X - 1))

    def ring_start(part):
        for half, step in turns:
            go(remote(sends.at[part, rows_of(2, half)], first.at[part, half], s_first.at[part, half], r_first.at[part, half], at_x(step)))
        for half, step in turns:
            go(remote(sends.at[part, rows_of(step, 1 - half)], alone.at[part, 1 - half], s_alone.at[part, half], r_alone.at[part, 1 - half], at_x(step)))

    def ring_join(part):
        for half, step in turns:
            landed(first.at[part, half], r_first.at[part, half])
            joint_out[part, half] = (first[part, half].astype(F32) + wide[part, rows_of(step, half)]).astype(BF)
            go(remote(joint_out.at[part, half], joined.at[part, half], s_joined.at[part, half], r_joined.at[part, half], at_x(step)))

    def along_z(part):
        for half in range(2):
            landed(alone.at[part, half], r_alone.at[part, half])
            landed(joined.at[part, half], r_joined.at[part, half])
            summed = wide[part, rows_of(0, half)] + alone[part, half].astype(F32) + joined[part, half].astype(F32)
            for k in range(HALF // Z_ROWS):
                z_out[part, half * (HALF // Z_ROWS) + k] = jnp.concatenate(
                    [summed[k * Z_ROWS : (k + 1) * Z_ROWS], jnp.zeros((Z_PAD - Z_ROWS, PIECE), F32)], axis=0
                ).astype(BF)
        for k in range(QUAD):
            place = core * QUAD + k
            copy = remote(z_out.at[part, k], z_in.at[part, z], s_z.at[part, k], r_z.at[part], at_z(place))
            go_or_copy(place == z, copy, z_out.at[part, k], z_in.at[part, z], r_z.at[part])

    spread(0)
    landed(left_in, r_left)
    multiply(0)
    ring_start(0)
    spread(1)
    ring_join(0)
    multiply(1)
    ring_start(1)
    along_z(0)
    ring_join(1)

    loads["w_qkv"].wait()
    landed(tok_in.at[0], r_tok.at[0])
    landed(tok_in.at[1], r_tok.at[1])
    mine = pl.ds(pl.multiple_of(core * ROWS, ROWS), ROWS)

    def tile_of(part, h):
        here = cols[part, low, h % GROUP, mine]
        return jnp.where(low == h // GROUP, here, tok_in[part, h % GROUP])

    qo = [tile_of(0, h) for h in range(HEADS)]
    kv_grads = [tile_of(1, h) for h in range(HEADS)]
    grad_qkv = jnp.concatenate(
        [tile[:, :HEAD_DIM] for tile in qo]
        + [tile[:, :HEAD_DIM] for tile in kv_grads]
        + [tile[:, HEAD_DIM:] for tile in kv_grads],
        axis=1,
    )
    grad_normed = lax.dot_general(grad_qkv, w_qkv[...], (((1,), (1,)), ((), ())), preferred_element_type=F32)
    standard = xhat[...]
    for row, terms in enumerate((jnp.sum(grad_normed * standard, axis=0, keepdims=True), jnp.sum(grad_normed, axis=0, keepdims=True))):
        for k in range(TILES):
            norm_mid[0, row * TILES + k : row * TILES + k + 1] = terms[:, k * 128 : (k + 1) * 128]
    norm_mid[0, 2 * TILES :] = jnp.zeros((NORM_ROWS - 2 * TILES, 128), F32)
    for step in range(1, N_Z):
        go(remote(norm_mid.at[0], norm_a.at[z], s_na.at[step], r_na, at_z(lax.rem(z + step, N_Z))))
    norm_a[z] = norm_mid[0]
    along_z(1)
    gx = grad_normed * gain_ref[...].reshape(1, D)
    grad_x = go_ref[...].astype(F32) + deviation[...] * (
        gx - jnp.mean(gx, axis=1, keepdims=True) - standard * jnp.mean(gx * standard, axis=1, keepdims=True)
    )
    stem_out[...] = (grad_x * slope[...]).astype(BF)
    stem_copy = pltpu.make_async_copy(stem_out, stem_hbm_out.at[0], s_load.at[7])
    stem_copy.start()

    landed(norm_a.at[pl.ds(0, N_Z - 1)], r_na)
    norm_mid[1] = jnp.sum(norm_a[...], axis=0)
    for step in range(1, N_X):
        go(remote(norm_mid.at[1], norm_b.at[x], s_nb.at[step], r_nb, at_x(step)))
    norm_b[x] = norm_mid[1]
    landed(norm_b.at[pl.ds(0, N_X - 1)], r_nb)
    norm_mid[2] = jnp.sum(norm_b[...], axis=0)
    for step in range(1, 2 * QUAD):
        go(remote(norm_mid.at[2], norm_c.at[mine8], s_nc.at[step], r_nc, at_eight(step)))
    norm_c[mine8] = norm_mid[2]

    holder = core == z // QUAD
    source = side * 2 + low

    def last_copy(step):
        place = lax.rem(lax.rem(mine8 + step, 2 * QUAD), QUAD)
        return remote(last_out.at[place], last_in.at[source], s_last.at[step], r_last, at_eight(step))

    @pl.when(holder)
    def _():
        for part in range(2):
            landed(z_in.at[part], r_z.at[part])
            summed = jnp.sum(z_in[part].astype(F32), axis=0)
            for place in range(QUAD):
                last_out[place, part] = jnp.concatenate(
                    [summed[place * OUT_ROWS : (place + 1) * OUT_ROWS], jnp.zeros((OUT_PAD - OUT_ROWS, PIECE), F32)], axis=0
                ).astype(BF)
        for step in range(1, 2 * QUAD):
            last_copy(step).start()
        pltpu.make_async_copy(last_out.at[t], last_in.at[source], r_last).start()

    landed(norm_c.at[pl.ds(0, 2 * QUAD - 1)], r_nc)
    norms = jnp.sum(norm_c[...], axis=0)
    for row in range(2):
        for k in range(TILES):
            norm_out[row : row + 1, k * 128 : (k + 1) * 128] = norms[row * TILES + k : row * TILES + k + 1]

    landed(last_in, r_last)
    quarters = [[], [], [], []]
    for g in range(2):
        both = last_in[g].astype(F32) + last_in[2 + g].astype(F32)
        for h in range(GROUP):
            for part, (a, b) in enumerate(((0, 3), (1, 2))):
                tile = both[part, :OUT_ROWS, h * PAIR : (h + 1) * PAIR]
                quarters[a].append(tile[:, :HEAD_DIM])
                quarters[b].append(tile[:, HEAD_DIM:])
    for k in range(4):
        out_ref[:, k * WIDTH : (k + 1) * WIDTH] = jnp.concatenate(quarters[k], axis=1)

    stem_copy.wait()
    for entry in pending:
        if isinstance(entry, tuple):
            pl.when(jnp.logical_not(entry[0]))(entry[1].wait_send)
        else:
            entry.wait_send()

    @pl.when(holder)
    def _():
        for step in range(1, 2 * QUAD):
            last_copy(step).wait_send()

    @pl.when(active)
    def _():
        def drain(i, carry):
            for buf, part, sem in ((ret_qo, 0, s_qo), (ret_kv, 1, s_dkv)):
                place, half, copy = back(buf, i, part, sem)
                pl.when(slot != place)(copy.wait_send)
            return carry

        lax.fori_loop(0, blocks, drain, 0)


def copy_kernel(a, b, c, a_out, b_out, c_out, a_mid, b_mid, c_mid, sems):
    routes = ((a, a_mid, a_out), (b, b_mid, b_out), (c, c_mid, c_out))
    inward = [pltpu.make_async_copy(src, mid, sems.at[0, index]) for index, (src, mid, dst) in enumerate(routes)]
    outward = [pltpu.make_async_copy(mid, dst, sems.at[1, index]) for index, (src, mid, dst) in enumerate(routes)]
    for copy in inward:
        copy.start()
    for first, second in zip(inward, outward):
        first.wait()
        second.start()
    for copy in outward:
        copy.wait()


def hand_on(*arrays):
    anywhere = pl.BlockSpec(memory_space=pl.ANY)
    return pl.pallas_call(
        copy_kernel,
        out_shape=tuple(jax.ShapeDtypeStruct(array.shape, array.dtype) for array in arrays),
        in_specs=[anywhere] * 3,
        out_specs=(anywhere,) * 3,
        scratch_shapes=[pltpu.VMEM(array.shape, array.dtype) for array in arrays] + [pltpu.SemaphoreType.DMA((2, 3))],
        compiler_params=pltpu.CompilerParams(vmem_limit_bytes=63 * 1024 * 1024),
        name="hand_on",
    )(*arrays)


def local(stem_pre, gain, bias, w_attn, queries, keys, values, grad_out, frames):
    vmem, dma = pltpu.VMEM, pltpu.SemaphoreType.DMA
    tile = (ROWS, PAIR)
    blocks = SEQ // BLOCK
    anywhere, inside = pl.BlockSpec(memory_space=pl.ANY), pl.BlockSpec(memory_space=vmem)
    results = pl.pallas_call(
        layer_kernel,
        out_shape=(
            jax.ShapeDtypeStruct((1, ROWS, D), BF),
            jax.ShapeDtypeStruct((OUT_ROWS, 4 * WIDTH), F32),
            jax.ShapeDtypeStruct((2, D), F32),
        ),
        in_specs=[anywhere, inside, inside, anywhere, anywhere, anywhere, anywhere, anywhere, pl.BlockSpec(memory_space=pltpu.SMEM)],
        out_specs=(anywhere, inside, inside),
        scratch_shapes=[
            vmem((ROWS, D), BF), vmem((D, WIDTH), BF), vmem((D, 3 * WIDTH), BF),
            vmem((ROWS, WIDTH), BF), vmem((ROWS, WIDTH), BF), vmem((ROWS, WIDTH), BF), vmem((ROWS, D), BF),
            vmem((HEADS,) + tile, BF), vmem((HEADS,) + tile, BF), vmem((SPAN,) + tile, BF), vmem((SPAN,) + tile, BF),
            vmem((blocks, BLOCK, PAIR), BF), vmem((blocks, BLOCK, PAIR), BF),
            vmem((SEQ, PAIR), BF), vmem((PAIR, SEQ), BF), vmem((SEQ, PAIR), F32), vmem((SEQ, BLOCK), F32), vmem((SEQ, BLOCK), BF),
            vmem((ROWS, D), F32), vmem((ROWS, D), F32), vmem((ROWS, 1), F32),
            vmem((2, 2, ROWS, D // 2), BF), vmem((QUAD, 2, ROWS, D // 2), BF),
            vmem((2, 2, GROUP, BLOCK, PAIR), BF), vmem((2, GROUP) + tile, BF),
            vmem((2, D // 2, PIECE), F32), vmem((2, D // 2, PIECE), BF),
            vmem((2, 2, HALF, PIECE), BF), vmem((2, 2, HALF, PIECE), BF), vmem((2, 2, HALF, PIECE), BF), vmem((2, 2, HALF, PIECE), BF),
            vmem((2, QUAD, Z_PAD, PIECE), BF), vmem((2, N_Z, Z_PAD, PIECE), BF),
            vmem((QUAD, 2, OUT_PAD, PIECE), BF), vmem((QUAD, 2, OUT_PAD, PIECE), BF),
            vmem((N_Z, NORM_ROWS, 128), F32), vmem((N_X, NORM_ROWS, 128), F32), vmem((2 * QUAD, NORM_ROWS, 128), F32),
            vmem((3, NORM_ROWS, 128), F32), vmem((ROWS, D), BF),
            dma((8,)), dma((HEADS,)), dma((HEADS,)), dma((blocks,)), dma((blocks,)), dma((QUAD,)), dma((2,)), dma((2, 2)),
            dma((2, 2)), dma((2, 2)), dma((2, 2)), dma((2, QUAD)), dma((2 * QUAD,)), dma((N_Z,)), dma((N_X,)), dma((2 * QUAD,)),
            dma, dma((blocks,)), dma((2,)), dma, dma((2,)), dma((2,)),
            dma((2, 2)), dma((2, 2)), dma((2, 2)), dma((2,)), dma, dma, dma, dma,
        ],
        compiler_params=pltpu.CompilerParams(
            collective_id=0, has_side_effects=True, vmem_limit_bytes=60 * 1024 * 1024
        ),
        name="layer_backward",
    )(stem_pre, gain, bias, w_attn, queries, keys, values, grad_out, frames)
    return hand_on(*results)


def solution(mesh):
    placed = (
        P("batch", "tm", None),
        P(),
        P(),
        P(),
        P("batch", "tm", None),
        P("batch", "tm", None),
        P("batch", "tm", None),
        P("batch", "tm", None),
        P("batch", None),
    )
    return jax.shard_map(
        local,
        mesh=mesh,
        in_specs=placed,
        out_specs=(P("batch", "tm", None), P("tm", None), P()),
        check_vma=False,
    )
```

```python
import math

import jax
import jax.numpy as jnp
from jax import lax
from jax.experimental import pallas as pl
from jax.experimental.pallas import tpu as pltpu
from jax.sharding import PartitionSpec as P

HEAD_DIM = 64
HEADS = 10
SPAN = 16
NEG_FILL = -1e30
EPSILON = 1e-05

OWNERS = (0, 4, 5, 8, 12, 2, 6, 10, 11, 14)
MESH = pl.DeviceIdType.MESH
D = 1280
WIDTH = HEADS * HEAD_DIM
PAIR = 2 * HEAD_DIM
GROUP = HEADS // 2
ROWS = 128
BLOCK = 256
SEQ = SPAN * ROWS
N_X, N_Z, QUAD = 4, 8, 4
PIECE = GROUP * PAIR
X_ROWS = 160
HALF = X_ROWS // 2
Z_ROWS = 40
Z_PAD = 48
OUT_ROWS = 10
OUT_PAD = 16
NORM_ROWS = 24
TILES = D // 128
CHUNK = 1024
BF, F32 = jnp.bfloat16, jnp.float32


def layer_kernel(
    stem_hbm, gain_ref, bias_ref, w_hbm, q_hbm, k_hbm, v_hbm, go_hbm, frames_ref,
    stem_hbm_out, out_ref, norm_out,
    stem_ref, w_out, w_qkv, q_ref, k_ref, v_ref, go_ref,
    kv_out, qd_out, kv_in, qd_in, ret_qo, ret_kv, masked_k, kv_t, total, scores, powers,
    xhat, slope, deviation, left_out, left_in, cols, tok_in,
    wide, sends, first, joined, alone, joint_out, z_out, z_in, last_out, last_in,
    norm_a, norm_b, norm_c, norm_mid, stem_out,
    s_load, s_kv, s_qd, s_qo, s_dkv, s_left, s_pair, s_tok, s_first, s_joined, s_alone, s_z, s_last,
    s_na, s_nb, s_nc,
    r_kv, r_qd, r_cols, r_left, r_pair, r_tok, r_first, r_joined, r_alone, r_z, r_last, r_na, r_nb, r_nc,
):
    me = lax.axis_index("tm")
    side = lax.axis_index("batch")
    slot = lax.rem(me, SPAN)
    base = me - slot
    core = lax.rem(me, 2)
    low = lax.rem(me // 2, 2)
    t = lax.rem(me, QUAD)
    z = lax.rem(me // QUAD, N_Z)
    x = me // (QUAD * N_Z)
    mine8 = side * QUAD + t

    loads = {}
    for index, (name, src, dst) in enumerate(
        (
            ("k", k_hbm.at[0], k_ref), ("v", v_hbm.at[0], v_ref), ("q", q_hbm.at[0], q_ref), ("go", go_hbm.at[0], go_ref),
            ("w_out", w_hbm.at[:, pl.ds(3 * WIDTH, WIDTH)], w_out), ("stem", stem_hbm.at[0], stem_ref),
            ("w_qkv", w_hbm.at[:, pl.ds(0, 3 * WIDTH)], w_qkv),
        )
    ):
        loads[name] = pltpu.make_async_copy(src, dst, s_load.at[index])
        loads[name].start()

    def at_x(step):
        return {"tm": lax.rem(x + step, N_X) * (QUAD * N_Z) + z * QUAD + t}

    def at_z(place):
        return {"tm": x * (QUAD * N_Z) + place * QUAD + t}

    def at_quad(place):
        return {"tm": x * (QUAD * N_Z) + z * QUAD + place}

    def at_eight(step):
        place = lax.rem(mine8 + step, 2 * QUAD)
        return {"tm": x * (QUAD * N_Z) + z * QUAD + lax.rem(place, QUAD), "batch": place // QUAD}

    def remote(src, dst, send_sem, recv_sem, device):
        return pltpu.make_async_remote_copy(
            src_ref=src, dst_ref=dst, send_sem=send_sem, recv_sem=recv_sem,
            device_id=device, device_id_type=MESH,
        )

    def landed(buf, sem):
        pltpu.make_async_copy(buf, buf, sem).wait()

    barrier = pltpu.get_barrier_semaphore()

    def greet(device):
        pl.semaphore_signal(barrier, inc=1, device_id=device, device_id_type=MESH)

    for step in range(1, SPAN):
        greet({"tm": base + lax.rem(slot + step, SPAN)})
    for step in range(1, N_X):
        greet(at_x(step))
    for place in range(QUAD):
        greet(at_z((1 - z // QUAD) * QUAD + place))
    for place in range(QUAD):
        greet({"tm": x * (QUAD * N_Z) + z * QUAD + place, "batch": 1 - side})

    pending = []

    def go(copy):
        copy.start()
        pending.append(copy)

    def go_or_copy(here, copy, src, dst, recv_sem, keep=True):
        pl.when(jnp.logical_not(here))(copy.start)
        pl.when(here)(pltpu.make_async_copy(src, dst, recv_sem).start)
        if keep:
            pending.append((here, copy))

    loads["k"].wait()
    loads["v"].wait()
    for h in range(HEADS):
        at = slice(h * HEAD_DIM, (h + 1) * HEAD_DIM)
        kv_out[h] = jnp.concatenate([k_ref[:, at], v_ref[:, at]], axis=1)
    pl.semaphore_wait(barrier, SPAN - 1 + N_X - 1 + 2 * QUAD)
    for h in range(HEADS):
        copy = remote(kv_out.at[h], kv_in.at[slot], s_kv.at[h], r_kv, {"tm": base + OWNERS[h]})
        go_or_copy(slot == OWNERS[h], copy, kv_out.at[h], kv_in.at[slot], r_kv)
    loads["q"].wait()
    loads["go"].wait()
    loads["w_out"].wait()
    grad_heads = jnp.dot(go_ref[...], w_out[...], preferred_element_type=F32).astype(BF)
    for h in range(HEADS):
        at = slice(h * HEAD_DIM, (h + 1) * HEAD_DIM)
        qd_out[h] = jnp.concatenate([q_ref[:, at], grad_heads[:, at]], axis=1)
    for h in range(HEADS):
        arrival = r_qd.at[slot // 2]
        copy = remote(qd_out.at[h], qd_in.at[slot], s_qd.at[h], arrival, {"tm": base + OWNERS[h]})
        go_or_copy(slot == OWNERS[h], copy, qd_out.at[h], qd_in.at[slot], arrival)

    loads["stem"].wait()
    stem_in = stem_ref[...].astype(F32)
    normal_cdf = 0.5 * (1.0 + lax.erf(stem_in / math.sqrt(2.0)))
    density = jnp.exp(-0.5 * stem_in * stem_in) / math.sqrt(2.0 * math.pi)
    slope[...] = normal_cdf + stem_in * density
    activated = stem_in * normal_cdf
    position = (slot * ROWS + lax.broadcasted_iota(jnp.int32, (ROWS, D // 2), 0)).astype(F32)
    feature = lax.broadcasted_iota(jnp.int32, (ROWS, D // 2), 1).astype(F32)
    angle = position * jnp.exp(-math.log(10000.0) / (D // 2 - 1) * feature)
    embedded = activated + jnp.concatenate([jnp.sin(angle), jnp.cos(angle)], axis=1)
    centered = embedded - jnp.mean(embedded, axis=1, keepdims=True)
    inverse = lax.rsqrt(jnp.mean(centered * centered, axis=1, keepdims=True) + EPSILON)
    standard = centered * inverse
    xhat[...] = standard
    deviation[...] = inverse
    normed = (standard * gain_ref[...].reshape(1, D) + bias_ref[...].reshape(1, D)).astype(BF)
    for kind, source in enumerate((normed, go_ref[...])):
        for r in range(2):
            left_out[r, kind] = jnp.concatenate(
                [source[:, c * 2 * X_ROWS + r * X_ROWS : c * 2 * X_ROWS + (r + 1) * X_ROWS] for c in range(N_X)], axis=1
            )
    for place in range(QUAD):
        copy = remote(left_out.at[place % 2], left_in.at[t], s_left.at[place], r_left, at_quad(place))
        go_or_copy(t == place, copy, left_out.at[place % 2], left_in.at[t], r_left)

    head = jnp.int32(0)
    active = jnp.bool_(False)
    for h in range(HEADS):
        head = jnp.where(slot == OWNERS[h], h % GROUP, head)
        active = jnp.logical_or(active, slot == OWNERS[h])
    blocks = SEQ // BLOCK

    def back(buf, index, part, send_sem):
        place = QUAD * (index // 2) + 2 * low + lax.rem(index, 2)
        half = lax.rem(index, 2)
        return place, half, remote(
            buf.at[index], cols.at[part, half, head], send_sem.at[index], r_cols.at[part], {"tm": base + place}
        )

    def send_back(buf, index, part, send_sem):
        place, half, copy = back(buf, index, part, send_sem)
        go_or_copy(slot == place, copy, buf.at[index], cols.at[part, half, head], r_cols.at[part], keep=False)

    @pl.when(active)
    def _():
        limit = frames_ref[0, me // SPAN]
        landed(kv_in, r_kv)
        kv = kv_in[...].reshape(SEQ, PAIR)
        lane = lax.broadcasted_iota(jnp.int32, kv.shape, 1)
        row = lax.broadcasted_iota(jnp.int32, kv.shape, 0)
        fill = jnp.where(jnp.logical_and(lane == HEAD_DIM, 2 * row >= limit), NEG_FILL, 0.0)
        masked_k[...] = jnp.where(lane < HEAD_DIM, kv.astype(F32), fill).astype(BF)
        kv_t[...] = kv.T
        total[...] = jnp.zeros_like(total)
        scale = 1.0 / math.sqrt(HEAD_DIM)
        blane = lax.broadcasted_iota(jnp.int32, (BLOCK, PAIR), 1)
        own = slot // QUAD

        def body(i, carry):
            step = i // 2
            step = jnp.where(step == 0, 0, jnp.where(step == 1, 2, jnp.where(step == 2, 3, 1)))
            near = lax.rem(own + step, 2) + 2 * lax.rem(own // 2 + step // 2, 2)
            at = 2 * near + lax.rem(i, 2)
            landed(qd_in.at[pl.ds(2 * at, 2)], r_qd.at[at])
            qd = qd_in[pl.ds(2 * at, 2)].reshape(BLOCK, PAIR).astype(F32)
            q_ones = jnp.where(blane < HEAD_DIM, qd * scale, jnp.where(blane == HEAD_DIM, 1.0, 0.0)).astype(BF)
            q_only = jnp.where(blane < HEAD_DIM, qd, 0.0).astype(BF)
            top = jnp.full((8, BLOCK), NEG_FILL, F32)
            for c in range(0, SEQ, CHUNK):
                part = lax.dot_general(
                    masked_k[c : c + CHUNK], q_ones, (((1,), (1,)), ((), ())), preferred_element_type=F32
                )
                scores[c : c + CHUNK] = part
                top = jnp.maximum(top, jnp.max(part.reshape(CHUNK // 8, 8, BLOCK), axis=0))
            top = jnp.max(top, axis=0, keepdims=True)
            mass = jnp.zeros((8, BLOCK), F32)
            attn_t = jnp.zeros((HEAD_DIM, BLOCK), F32)
            for c in range(0, SEQ, CHUNK):
                power = jnp.exp(scores[c : c + CHUNK] - top)
                mass = mass + jnp.sum(power.reshape(CHUNK // 8, 8, BLOCK), axis=0)
                power_b = power.astype(BF)
                powers[c : c + CHUNK] = power_b
                attn_t = attn_t + jnp.dot(kv_t[HEAD_DIM:, c : c + CHUNK], power_b, preferred_element_type=F32)
            inverse_mass = 1.0 / jnp.sum(mass, axis=0, keepdims=True)
            attn_t = (attn_t * inverse_mass).astype(BF).astype(F32)
            shared_t = qd.T[HEAD_DIM:] * inverse_mass
            shared = jnp.concatenate([jnp.zeros((HEAD_DIM, BLOCK), F32), shared_t], axis=0).T
            d_only = shared.astype(BF)
            d_scaled = (shared * scale).astype(BF)
            delta = scale * jnp.sum(shared_t.astype(BF).astype(F32) * attn_t, axis=0, keepdims=True)
            dq_t = jnp.zeros((HEAD_DIM, BLOCK), F32)
            for c in range(0, SEQ, CHUNK):
                grad_prob = lax.dot_general(
                    kv_in[c // ROWS : (c + CHUNK) // ROWS].reshape(CHUNK, PAIR), d_scaled, (((1,), (1,)), ((), ())),
                    preferred_element_type=F32,
                )
                power_b = powers[c : c + CHUNK]
                dscore = (power_b.astype(F32) * (grad_prob - delta)).astype(BF)
                dq_t = dq_t + jnp.dot(kv_t[:HEAD_DIM, c : c + CHUNK], dscore, preferred_element_type=F32)
                total[c : c + CHUNK] += jnp.dot(dscore, q_only, preferred_element_type=F32) + jnp.dot(
                    power_b, d_only, preferred_element_type=F32
                )
            ret_qo[at] = jnp.concatenate([dq_t, attn_t], axis=0).T.astype(BF)
            send_back(ret_qo, at, 0, s_qo)
            return carry

        lax.fori_loop(0, blocks, body, 0)
        ret_kv[...] = total[...].astype(BF).reshape(blocks, BLOCK, PAIR)

        def send_kv_grads(i, carry):
            step = i // 2
            step = jnp.where(step == 0, 2, jnp.where(step == 1, 3, jnp.where(step == 2, 1, 0)))
            near = lax.rem(own + step, 2) + 2 * lax.rem(own // 2 + step // 2, 2)
            send_back(ret_kv, 2 * near + lax.rem(i, 2), 1, s_dkv)
            return carry

        lax.fori_loop(0, blocks, send_kv_grads, 0)

    def spread(part):
        landed(cols.at[part, core], r_cols.at[part])
        go(remote(cols.at[part, core], cols.at[part, core], s_pair.at[part], r_pair.at[part], at_quad(2 * low + 1 - core)))
        for k in range(2):
            copy = remote(
                cols.at[part, core, :, pl.ds(k * ROWS, ROWS)], tok_in.at[part], s_tok.at[part, k], r_tok.at[part],
                at_quad(2 * core + k),
            )
            pl.when(core != low)(copy.start)
            pending.append((core == low, copy))

    tokens = QUAD * ROWS

    def rows_of(step, half):
        chunk = lax.rem(x + step, N_X)
        return pl.ds(pl.multiple_of(chunk * X_ROWS + half * HALF, 16), HALF)

    def multiply(part):
        landed(cols.at[part, 1 - core], r_pair.at[part])
        right = jnp.concatenate([cols[part, :, h].reshape(tokens, PAIR) for h in range(GROUP)], axis=1)
        even = lax.rem(lax.broadcasted_iota(jnp.int32, (128, PIECE), 1), PAIR) < HEAD_DIM
        for at in range(0, PIECE, 128):
            product = lax.dot_general(
                left_in[:, 0, :, at : at + 128].reshape(tokens, 128), right, (((0,), (0,)), ((), ())),
                preferred_element_type=F32,
            )
            if part == 0:
                other = lax.dot_general(
                    left_in[:, 1, :, at : at + 128].reshape(tokens, 128), right, (((0,), (0,)), ((), ())),
                    preferred_element_type=F32,
                )
                product = jnp.where(even, product, other)
            wide[part, at : at + 128] = product
            sends[part, at : at + 128] = product.astype(BF)

    turns = ((0, 1), (1, N_X - 1))

    def ring_start(part):
        for half, step in turns:
            go(remote(sends.at[part, rows_of(2, half)], first.at[part, half], s_first.at[part, half], r_first.at[part, half], at_x(step)))
        for half, step in turns:
            go(remote(sends.at[part, rows_of(step, 1 - half)], alone.at[part, 1 - half], s_alone.at[part, half], r_alone.at[part, 1 - half], at_x(step)))

    def ring_join(part):
        for half, step in turns:
            landed(first.at[part, half], r_first.at[part, half])
            joint_out[part, half] = (first[part, half].astype(F32) + wide[part, rows_of(step, half)]).astype(BF)
            go(remote(joint_out.at[part, half], joined.at[part, half], s_joined.at[part, half], r_joined.at[part, half], at_x(step)))

    def along_z(part):
        for half in range(2):
            landed(alone.at[part, half], r_alone.at[part, half])
            landed(joined.at[part, half], r_joined.at[part, half])
            summed = wide[part, rows_of(0, half)] + alone[part, half].astype(F32) + joined[part, half].astype(F32)
            for k in range(HALF // Z_ROWS):
                z_out[part, half * (HALF // Z_ROWS) + k] = jnp.concatenate(
                    [summed[k * Z_ROWS : (k + 1) * Z_ROWS], jnp.zeros((Z_PAD - Z_ROWS, PIECE), F32)], axis=0
                ).astype(BF)
        for k in range(QUAD):
            place = core * QUAD + k
            copy = remote(z_out.at[part, k], z_in.at[part, z], s_z.at[part, k], r_z.at[part], at_z(place))
            go_or_copy(place == z, copy, z_out.at[part, k], z_in.at[part, z], r_z.at[part])

    spread(0)
    landed(left_in, r_left)
    multiply(0)
    ring_start(0)
    spread(1)
    ring_join(0)
    multiply(1)
    ring_start(1)

    loads["w_qkv"].wait()
    landed(tok_in.at[0], r_tok.at[0])
    landed(tok_in.at[1], r_tok.at[1])
    mine = pl.ds(pl.multiple_of(core * ROWS, ROWS), ROWS)

    def tile_of(part, h):
        here = cols[part, low, h % GROUP, mine]
        return jnp.where(low == h // GROUP, here, tok_in[part, h % GROUP])

    qo = [tile_of(0, h) for h in range(HEADS)]
    kv_grads = [tile_of(1, h) for h in range(HEADS)]
    grad_qkv = jnp.concatenate(
        [tile[:, :HEAD_DIM] for tile in qo]
        + [tile[:, :HEAD_DIM] for tile in kv_grads]
        + [tile[:, HEAD_DIM:] for tile in kv_grads],
        axis=1,
    )
    grad_normed = lax.dot_general(grad_qkv, w_qkv[...], (((1,), (1,)), ((), ())), preferred_element_type=F32)
    standard = xhat[...]
    for row, terms in enumerate((jnp.sum(grad_normed * standard, axis=0, keepdims=True), jnp.sum(grad_normed, axis=0, keepdims=True))):
        for k in range(TILES):
            norm_mid[0, row * TILES + k : row * TILES + k + 1] = terms[:, k * 128 : (k + 1) * 128]
    norm_mid[0, 2 * TILES :] = jnp.zeros((NORM_ROWS - 2 * TILES, 128), F32)
    for step in range(1, N_Z):
        go(remote(norm_mid.at[0], norm_a.at[z], s_na.at[step], r_na, at_z(lax.rem(z + step, N_Z))))
    norm_a[z] = norm_mid[0]
    along_z(0)
    ring_join(1)
    gx = grad_normed * gain_ref[...].reshape(1, D)
    grad_x = go_ref[...].astype(F32) + deviation[...] * (
        gx - jnp.mean(gx, axis=1, keepdims=True) - standard * jnp.mean(gx * standard, axis=1, keepdims=True)
    )
    stem_out[...] = (grad_x * slope[...]).astype(BF)
    stem_copy = pltpu.make_async_copy(stem_out, stem_hbm_out.at[0], s_load.at[7])
    stem_copy.start()
    along_z(1)

    landed(norm_a.at[pl.ds(0, N_Z - 1)], r_na)
    norm_mid[1] = jnp.sum(norm_a[...], axis=0)
    for step in range(1, N_X):
        go(remote(norm_mid.at[1], norm_b.at[x], s_nb.at[step], r_nb, at_x(step)))
    norm_b[x] = norm_mid[1]
    landed(norm_b.at[pl.ds(0, N_X - 1)], r_nb)
    norm_mid[2] = jnp.sum(norm_b[...], axis=0)
    for step in range(1, 2 * QUAD):
        go(remote(norm_mid.at[2], norm_c.at[mine8], s_nc.at[step], r_nc, at_eight(step)))
    norm_c[mine8] = norm_mid[2]

    holder = core == z // QUAD
    source = side * 2 + low

    def last_copy(step):
        place = lax.rem(lax.rem(mine8 + step, 2 * QUAD), QUAD)
        return remote(last_out.at[place], last_in.at[source], s_last.at[step], r_last, at_eight(step))

    @pl.when(holder)
    def _():
        for part in range(2):
            landed(z_in.at[part], r_z.at[part])
            summed = jnp.sum(z_in[part].astype(F32), axis=0)
            for place in range(QUAD):
                last_out[place, part] = jnp.concatenate(
                    [summed[place * OUT_ROWS : (place + 1) * OUT_ROWS], jnp.zeros((OUT_PAD - OUT_ROWS, PIECE), F32)], axis=0
                ).astype(BF)
        for step in range(1, 2 * QUAD):
            last_copy(step).start()
        pltpu.make_async_copy(last_out.at[t], last_in.at[source], r_last).start()

    landed(norm_c.at[pl.ds(0, 2 * QUAD - 1)], r_nc)
    norms = jnp.sum(norm_c[...], axis=0)
    for row in range(2):
        for k in range(TILES):
            norm_out[row : row + 1, k * 128 : (k + 1) * 128] = norms[row * TILES + k : row * TILES + k + 1]

    landed(last_in, r_last)
    quarters = [[], [], [], []]
    for g in range(2):
        both = last_in[g].astype(F32) + last_in[2 + g].astype(F32)
        for h in range(GROUP):
            for part, (a, b) in enumerate(((0, 3), (1, 2))):
                tile = both[part, :OUT_ROWS, h * PAIR : (h + 1) * PAIR]
                quarters[a].append(tile[:, :HEAD_DIM])
                quarters[b].append(tile[:, HEAD_DIM:])
    for k in range(4):
        out_ref[:, k * WIDTH : (k + 1) * WIDTH] = jnp.concatenate(quarters[k], axis=1)

    stem_copy.wait()
    for entry in pending:
        if isinstance(entry, tuple):
            pl.when(jnp.logical_not(entry[0]))(entry[1].wait_send)
        else:
            entry.wait_send()

    @pl.when(holder)
    def _():
        for step in range(1, 2 * QUAD):
            last_copy(step).wait_send()

    @pl.when(active)
    def _():
        def drain(i, carry):
            for buf, part, sem in ((ret_qo, 0, s_qo), (ret_kv, 1, s_dkv)):
                place, half, copy = back(buf, i, part, sem)
                pl.when(slot != place)(copy.wait_send)
            return carry

        lax.fori_loop(0, blocks, drain, 0)


def copy_kernel(a, b, c, a_out, b_out, c_out, a_mid, b_mid, c_mid, sems):
    routes = ((a, a_mid, a_out), (b, b_mid, b_out), (c, c_mid, c_out))
    inward = [pltpu.make_async_copy(src, mid, sems.at[0, index]) for index, (src, mid, dst) in enumerate(routes)]
    outward = [pltpu.make_async_copy(mid, dst, sems.at[1, index]) for index, (src, mid, dst) in enumerate(routes)]
    for copy in inward:
        copy.start()
    for first, second in zip(inward, outward):
        first.wait()
        second.start()
    for copy in outward:
        copy.wait()


def hand_on(*arrays):
    anywhere = pl.BlockSpec(memory_space=pl.ANY)
    return pl.pallas_call(
        copy_kernel,
        out_shape=tuple(jax.ShapeDtypeStruct(array.shape, array.dtype) for array in arrays),
        in_specs=[anywhere] * 3,
        out_specs=(anywhere,) * 3,
        scratch_shapes=[pltpu.VMEM(array.shape, array.dtype) for array in arrays] + [pltpu.SemaphoreType.DMA((2, 3))],
        compiler_params=pltpu.CompilerParams(vmem_limit_bytes=63 * 1024 * 1024),
        name="hand_on",
    )(*arrays)


def local(stem_pre, gain, bias, w_attn, queries, keys, values, grad_out, frames):
    vmem, dma = pltpu.VMEM, pltpu.SemaphoreType.DMA
    tile = (ROWS, PAIR)
    blocks = SEQ // BLOCK
    anywhere, inside = pl.BlockSpec(memory_space=pl.ANY), pl.BlockSpec(memory_space=vmem)
    results = pl.pallas_call(
        layer_kernel,
        out_shape=(
            jax.ShapeDtypeStruct((1, ROWS, D), BF),
            jax.ShapeDtypeStruct((OUT_ROWS, 4 * WIDTH), F32),
            jax.ShapeDtypeStruct((2, D), F32),
        ),
        in_specs=[anywhere, inside, inside, anywhere, anywhere, anywhere, anywhere, anywhere, pl.BlockSpec(memory_space=pltpu.SMEM)],
        out_specs=(anywhere, inside, inside),
        scratch_shapes=[
            vmem((ROWS, D), BF), vmem((D, WIDTH), BF), vmem((D, 3 * WIDTH), BF),
            vmem((ROWS, WIDTH), BF), vmem((ROWS, WIDTH), BF), vmem((ROWS, WIDTH), BF), vmem((ROWS, D), BF),
            vmem((HEADS,) + tile, BF), vmem((HEADS,) + tile, BF), vmem((SPAN,) + tile, BF), vmem((SPAN,) + tile, BF),
            vmem((blocks, BLOCK, PAIR), BF), vmem((blocks, BLOCK, PAIR), BF),
            vmem((SEQ, PAIR), BF), vmem((PAIR, SEQ), BF), vmem((SEQ, PAIR), F32), vmem((SEQ, BLOCK), F32), vmem((SEQ, BLOCK), BF),
            vmem((ROWS, D), F32), vmem((ROWS, D), F32), vmem((ROWS, 1), F32),
            vmem((2, 2, ROWS, D // 2), BF), vmem((QUAD, 2, ROWS, D // 2), BF),
            vmem((2, 2, GROUP, BLOCK, PAIR), BF), vmem((2, GROUP) + tile, BF),
            vmem((2, D // 2, PIECE), F32), vmem((2, D // 2, PIECE), BF),
            vmem((2, 2, HALF, PIECE), BF), vmem((2, 2, HALF, PIECE), BF), vmem((2, 2, HALF, PIECE), BF), vmem((2, 2, HALF, PIECE), BF),
            vmem((2, QUAD, Z_PAD, PIECE), BF), vmem((2, N_Z, Z_PAD, PIECE), BF),
            vmem((QUAD, 2, OUT_PAD, PIECE), BF), vmem((QUAD, 2, OUT_PAD, PIECE), BF),
            vmem((N_Z, NORM_ROWS, 128), F32), vmem((N_X, NORM_ROWS, 128), F32), vmem((2 * QUAD, NORM_ROWS, 128), F32),
            vmem((3, NORM_ROWS, 128), F32), vmem((ROWS, D), BF),
            dma((8,)), dma((HEADS,)), dma((HEADS,)), dma((blocks,)), dma((blocks,)), dma((QUAD,)), dma((2,)), dma((2, 2)),
            dma((2, 2)), dma((2, 2)), dma((2, 2)), dma((2, QUAD)), dma((2 * QUAD,)), dma((N_Z,)), dma((N_X,)), dma((2 * QUAD,)),
            dma, dma((blocks,)), dma((2,)), dma, dma((2,)), dma((2,)),
            dma((2, 2)), dma((2, 2)), dma((2, 2)), dma((2,)), dma, dma, dma, dma,
        ],
        compiler_params=pltpu.CompilerParams(
            collective_id=0, has_side_effects=True, vmem_limit_bytes=60 * 1024 * 1024
        ),
        name="layer_backward",
    )(stem_pre, gain, bias, w_attn, queries, keys, values, grad_out, frames)
    return hand_on(*results)


def solution(mesh):
    placed = (
        P("batch", "tm", None),
        P(),
        P(),
        P(),
        P("batch", "tm", None),
        P("batch", "tm", None),
        P("batch", "tm", None),
        P("batch", "tm", None),
        P("batch", None),
    )
    return jax.shard_map(
        local,
        mesh=mesh,
        in_specs=placed,
        out_specs=(P("batch", "tm", None), P("tm", None), P()),
        check_vma=False,
    )
```
